1024 devices in a mesh: expert: 64 (over z, y), dp: 16 (over x, core).
Axes of the slice: x: 8, y: 8, z: 8, core: 2. Of those that a mesh axis runs over, the one named last changes fastest.
Arguments:
- grad_out: bfloat16 [16, 8192, 2048], P('dp', 'expert'), may hold values from -6 to 6
- router_logits: float32 [16, 8192, 64], P('dp', 'expert'), may hold values from -8 to 8
- choices: int32 [16, 64, 256], P('dp'), may hold values from 0 to 8191, as said below
- pre_act: bfloat16 [16, 64, 256, 1024], P('dp', 'expert'), may hold values from -6 to 6
- w_down: bfloat16 [64, 1024, 2048], P('expert'), may hold values from -0.125 to 0.125
- w_up: bfloat16 [64, 2048, 1024], P('expert'), may hold values from -0.1875 to 0.1875
Outputs:
- grad_tokens: bfloat16 [16, 8192, 2048], P('dp', 'expert')
- grad_logits: float32 [16, 8192, 64], P('dp', 'expert')
- down_grad: bfloat16 [64, 1024, 2048], P('expert', 'dp')
The draws below stay inside these ranges and needn't reach their ends.
Inputs may be any that keep to these rules, and one draw needn't show every extreme that they name: Each block choices[g, e, :] lists 256 different tokens of group g. Of one block, at most 6 tokens lie in one device's tokens j * 128 to (j + 1) * 128 - 1, and in every block some device supplies exactly 6.
All inputs are finite; a program needn't handle non-finite values.
Results may differ from the reference program's by a relative error of at most 0.022.
Values may be sent and summed in bfloat16 or wider, within the bound.
A program may use at most 64 MiB of HBM per device.

```python
import jax
import jax.numpy as jnp
from jax import lax

D = 2048
FF = 1024
TOK_DEV = 128
EXPERTS = 64
GROUPS = 16
GROUP_TOK = 8192
CAP = 256
LOAD = 4
N_EXPERT = 64


def distinct_order(key, lead_shape, length):
    scores = jax.random.randint(key, lead_shape + (length,), 0, 1 << 16) * length + jnp.arange(length, dtype=jnp.int32)
    return jnp.argsort(scores, axis=-1).astype(jnp.int32)


def draw_choices(key, part):
    key = jax.random.fold_in(key, 7)
    owner_count = N_EXPERT
    group_count = GROUPS
    expert_count = EXPERTS
    half_load = LOAD // 2
    keys_all = jax.random.split(key, 6)
    order = distinct_order(keys_all[0], (group_count, expert_count), owner_count)
    hot_rank = jnp.argsort(distinct_order(keys_all[1], (group_count,), owner_count), axis=-1).astype(jnp.int32)
    shifts = jax.random.randint(keys_all[2], (group_count, expert_count, owner_count // 2), 0, half_load + 1)
    shifts = shifts.at[:, :, 0].set(half_load)
    position = jnp.arange(owner_count, dtype=jnp.int32)
    partner = jnp.bitwise_xor(position, 1)
    partner_owner = order[:, :, partner]
    rank_full = jnp.broadcast_to(hot_rank[:, None, :], order.shape)
    rank_self = jnp.take_along_axis(rank_full, order, axis=2)
    rank_other = jnp.take_along_axis(rank_full, partner_owner, axis=2)
    signed = jnp.where(rank_self > rank_other, 1, -1)
    amount = LOAD + signed * shifts[:, :, position // 2]
    counts = jnp.take_along_axis(amount, jnp.argsort(order, axis=2), axis=2)
    offsets = jnp.cumsum(counts, axis=1) - counts
    ends = jnp.cumsum(counts, axis=2)
    begins = ends - counts
    slot_ids = jnp.arange(CAP, dtype=jnp.int32)
    owner_of = jnp.sum((ends[:, :, None, :] <= slot_ids[None, None, :, None]).astype(jnp.int32), axis=3)
    within = slot_ids[None, None, :] - jnp.take_along_axis(begins, owner_of, axis=2)
    offset_at = jnp.take_along_axis(offsets, owner_of, axis=2)
    wheel = distinct_order(keys_all[3], (group_count, owner_count), TOK_DEV)
    starts = jax.random.randint(keys_all[4], (group_count, owner_count), 0, TOK_DEV)
    group_ids = jnp.arange(group_count, dtype=jnp.int32)[:, None, None]
    start_at = starts[group_ids, owner_of]
    place = (start_at + offset_at + within) % TOK_DEV
    local_tok = wheel[group_ids, owner_of, place]
    tokens = owner_of * TOK_DEV + local_tok
    shuffle = distinct_order(keys_all[5], (group_count, expert_count), CAP)
    return jnp.take_along_axis(tokens, shuffle, axis=2).astype(jnp.int32)


def raised(result, stream_key, source, target, shards_of, factor):
    owner, partner = [(jnp.arange(result.shape[dim]) // (result.shape[dim] // shards_of)).reshape([-1 if axis == dim else 1 for axis in range(result.ndim)]) for dim in (source, target)]
    chosen = jax.random.permutation(stream_key, shards_of)[partner]
    strong = (owner == chosen) | (owner == (partner + shards_of // 2) % shards_of)
    return jnp.where(strong, factor * result, result)


def block_scale(own_key, extent, shards, smallest, high):
    def one(dim, shards_of):
        heights = jax.random.uniform(jax.random.fold_in(jax.random.fold_in(own_key, 6), dim), (shards_of,), jnp.float32, smallest / len(shards), high / len(shards))
        return jnp.repeat(jnp.exp(heights), extent[dim] // shards_of).reshape((-1,) + (1,) * (len(extent) - dim - 1))

    loudness = one(*shards[0])
    for cut in shards[1:]:
        loudness = loudness * one(*cut)
    return loudness


def gaussian(key, dims, scale, reach, cuts=(), held_as=jnp.bfloat16):
    level = block_scale(key, dims, cuts, -0.22, 0.18) if cuts else 1.0
    result = jax.random.normal(key, dims, jnp.float32) * scale * level
    return jnp.minimum(jnp.maximum(result, -reach), reach).astype(held_as)


def noise_with(stream_key, dims, spread, reach, shards, heavy, kind=jnp.bfloat16):
    result = spread * jax.random.normal(stream_key, dims, jnp.float32)
    if shards:
        result = result * block_scale(stream_key, dims, shards, -0.22, 0.18)
    return jnp.clip(raised(result, jax.random.fold_in(stream_key, 3), *heavy), -reach, reach).astype(kind)


def setup_inputs(seed: int = 0) -> dict:
    keys = jax.random.split(jax.random.key(seed), 7)
    grad_out = gaussian(keys[0], (GROUPS, GROUP_TOK, D), 1.0, 6.0, ((0, 16), (1, 64)))
    router_logits = gaussian(keys[1], (GROUPS, GROUP_TOK, EXPERTS), 2.0, 8.0, ((0, 16), (1, 64)), jnp.float32)
    choices = draw_choices(jax.random.fold_in(keys[6], 71), 0)
    pre_act = noise_with(keys[3], (GROUPS, EXPERTS, CAP, FF), 1.0, 6.0, ((0, 16), (1, 64)), (0, 3, 16, 2.0))
    w_down = gaussian(keys[4], (EXPERTS, FF, D), D ** -0.5, 0.125, ((0, 64),))
    w_up = gaussian(keys[5], (EXPERTS, D, FF), FF ** -0.5, 0.1875, ((0, 64),))
    return dict(grad_out=grad_out, router_logits=router_logits, choices=choices, pre_act=pre_act, w_down=w_down, w_up=w_up)


ROOT_TWO_PI = 0.7978845608028654
CUBIC = 0.044715


def gelu_pair(values):
    inner_arg = ROOT_TWO_PI * (values + CUBIC * values * values * values)
    tanh_part = jnp.tanh(inner_arg)
    hidden = 0.5 * values * (1.0 + tanh_part)
    slope_vals = 0.5 * (1.0 + tanh_part) + 0.5 * values * (1.0 - tanh_part * tanh_part) * ROOT_TWO_PI * (1.0 + 3.0 * CUBIC * values * values)
    return hidden, slope_vals


def expert_backward(picked_rows, gate_sent, act_block, down_matrix, up_matrix):
    back_grad = jnp.dot(picked_rows, down_matrix.T, preferred_element_type=jnp.float32)
    hidden, slope_vals = gelu_pair(act_block.astype(jnp.float32))
    gate_grad = jnp.sum(back_grad * hidden, axis=1).astype(jnp.bfloat16)
    gate_col = gate_sent.astype(jnp.float32)[:, None]
    pre_grad = (gate_col * back_grad * slope_vals).astype(jnp.bfloat16)
    scaled = (gate_col * picked_rows.astype(jnp.float32)).astype(jnp.bfloat16)
    partial_value = jnp.dot(hidden.astype(jnp.bfloat16).T, scaled, preferred_element_type=jnp.float32).astype(jnp.bfloat16)
    token_rows = jnp.dot(pre_grad, up_matrix.T, preferred_element_type=jnp.float32).astype(jnp.bfloat16)
    return token_rows, gate_grad, partial_value


def reference(grad_out, router_logits, choices, pre_act, w_down, w_up):
    expert_ids = jnp.arange(EXPERTS, dtype=jnp.int32)[:, None]

    def per_expert(pieces):
        return expert_backward(pieces[0], pieces[1], pieces[2], pieces[3], pieces[4])

    def one_group(running, inputs):
        grad_rows, logit_rows, picked, act_block = inputs
        gate_vals = jax.nn.sigmoid(logit_rows)
        gate_sent = gate_vals[picked, expert_ids].astype(jnp.bfloat16)
        picked_rows = grad_rows[picked]
        token_rows, gate_grad, partial_value = lax.map(per_expert, (picked_rows, gate_sent, act_block, w_down, w_up))
        running = running + lax.optimization_barrier(partial_value).astype(jnp.float32)
        flat_tok = picked.reshape(-1)
        summed = jnp.zeros((GROUP_TOK, D), jnp.float32).at[flat_tok].add(token_rows.reshape(-1, D).astype(jnp.float32))
        expert_grid = jnp.broadcast_to(expert_ids, picked.shape)
        logit_grad = jnp.zeros((GROUP_TOK, EXPERTS), jnp.float32).at[picked, expert_grid].add(gate_grad.astype(jnp.float32))
        return running, (summed.astype(jnp.bfloat16), logit_grad * gate_vals * (1.0 - gate_vals))

    initial = jnp.zeros((EXPERTS, FF, D), jnp.float32)
    running, outputs = lax.scan(one_group, initial, (grad_out, router_logits, choices, pre_act))
    return outputs[0], outputs[1], running.astype(jnp.bfloat16)
```

```python
import jax
import jax.numpy as jnp
from jax import lax
from jax.experimental import pallas as pl
from jax.experimental.pallas import tpu as pltpu
from jax.sharding import PartitionSpec as P

ROOT_TWO_PI = 0.7978845608028654
CUBIC = 0.044715
MESH = pl.DeviceIdType.MESH

SIDE = 8
PEERS = 64
RING = 8
TOK = 128
WIDTH = 2048
FF = 1024
CAP = 256
SLOTS = 6
FLAT = PEERS * SLOTS
SUB = 16
GROUP = 16
GROUPS = PEERS // GROUP
ROWS = GROUP * SLOTS
BLOCK = FF // (2 * RING)
HALF = BLOCK // 2

F32 = jnp.float32
BF16 = jnp.bfloat16
I32 = jnp.int32


def contract(left, right, left_dim, right_dim):
    return lax.dot_general(
        left, right, (((left_dim,), (right_dim,)), ((), ())), preferred_element_type=F32
    )


def gelu_pair(values):
    inner_arg = ROOT_TWO_PI * (values + CUBIC * values * values * values)
    tanh_part = jnp.tanh(inner_arg)
    hidden = 0.5 * values * (1.0 + tanh_part)
    slope_vals = 0.5 * (1.0 + tanh_part) + 0.5 * values * (
        1.0 - tanh_part * tanh_part
    ) * ROOT_TWO_PI * (1.0 + 3.0 * CUBIC * values * values)
    return hidden, slope_vals


def iota(shape, dim):
    return lax.broadcasted_iota(I32, shape, dim)


def kernel(
    choices_ref, logits_ref, rows_ref, act_ref, down_hbm, up_hbm,
    tok_out, logit_out, down_out,
    w_down, w_up, stage, send_buf, recv_buf, back_buf, ret_buf,
    gate_send, gate_recv, grad_send, grad_recv,
    landing, tok_of_row, rows2d, scaled, hidden, slope, hidden_t, pre_grad,
    partial, pair_recv, pair_sum, ring_send, ring_recv,
    weight_sem,
    send_sem, recv_sem, gate_send_sem, gate_recv_sem,
    back_send_sem, back_recv_sem, grad_send_sem, grad_recv_sem,
    pair_send_sem, pair_recv_sem, ring_send_sem, ring_recv_sem,
):
    me = lax.axis_index("expert")
    data = lax.axis_index("dp")
    my_z, my_y = lax.div(me, SIDE), lax.rem(me, SIDE)
    my_x, core = lax.div(data, 2), lax.rem(data, 2)
    sign = 1 - 2 * core

    def partner(step, way):
        dz = lax.rem(3 * step, SIDE)
        dy = lax.rem(2 * step + lax.div(step, SIDE), SIDE)
        z = lax.rem(my_z + way * dz + SIDE, SIDE)
        y = lax.rem(my_y + way * dy + SIDE, SIDE)
        return z * SIDE + y

    def step_between(origin, target):
        dz = jnp.bitwise_and(sign * ((target >> 3) - (origin >> 3)), SIDE - 1)
        dy = jnp.bitwise_and(sign * ((target & 7) - (origin & 7)), SIDE - 1)
        low = jnp.bitwise_and(3 * dz, SIDE - 1)
        return jnp.bitwise_and(dy - 2 * low, SIDE - 1) * SIDE + low

    right = lax.rem(my_x + 1, RING) * 2 + core
    left = lax.rem(my_x + RING - 1, RING) * 2 + core
    sibling = my_x * 2 + 1 - core

    copy_down = pltpu.make_async_copy(down_hbm, w_down, weight_sem.at[0])
    copy_up = pltpu.make_async_copy(up_hbm, w_up, weight_sem.at[1])
    copy_down.start()
    copy_up.start()

    barrier = pltpu.get_barrier_semaphore()

    def greet(step, carry):
        pl.semaphore_signal(
            barrier, inc=1, device_id={"expert": lax.rem(me + step, PEERS)}, device_id_type=MESH
        )
        return carry

    lax.fori_loop(1, PEERS, greet, 0)
    for other in (left, right, sibling):
        pl.semaphore_signal(barrier, inc=1, device_id={"dp": other}, device_id_type=MESH)

    chosen = choices_ref[...]
    mine = (chosen >> 7) == me
    token = jnp.where(mine, (chosen & (TOK - 1)) + 1, 0)
    lane = iota((PEERS, CAP), 1)
    before = jnp.where(mine, 1, 0)
    shift = 1
    while shift < CAP:
        before = before + jnp.where(lane >= shift, pltpu.roll(before, shift, 1), 0)
        shift *= 2
    column = iota((PEERS, GROUPS * 128), 1)
    within = column & 127
    step_in = (within * 43) >> 8
    slot_in = within - SLOTS * step_in
    at_step = step_between(me, iota((PEERS, GROUPS * 128), 0)) == (column >> 7) * GROUP + step_in
    at_step = at_step & (within < ROWS)
    spread = jnp.zeros((PEERS, GROUPS * 128), I32)
    for k in range(SLOTS):
        token_k = jnp.sum(jnp.where(before == k + 1, token, 0), axis=1, keepdims=True)
        spread = spread + jnp.where(at_step & (slot_in == k), token_k, 0)
    token_row = jnp.sum(spread, axis=0, keepdims=True) - 1
    landing_f = jnp.where(token_row == iota((TOK, GROUPS * 128), 0), 1.0, 0.0)
    landing[...] = landing_f.astype(BF16)

    expert_step = step_between(me, iota((PEERS, PEERS), 0)) == iota((PEERS, PEERS), 1)
    expert_to_step = jnp.where(expert_step, 1.0, 0.0).astype(BF16)
    eye = jnp.where(iota((TOK, TOK), 0) == iota((TOK, TOK), 1), 1.0, 0.0).astype(BF16)
    gates = 1.0 / (1.0 + jnp.exp(-logits_ref[...]))
    by_step = jnp.dot(gates.astype(BF16), expert_to_step, preferred_element_type=F32)
    gate_send[:, 0, :] = contract(by_step.astype(BF16), eye, 0, 0)

    def tiles(row, count):
        return pl.ds(pl.multiple_of(row * SUB, SUB), count * SUB)

    def gather(g):
        pick = jnp.transpose(landing_f[:, g * 128:(g + 1) * 128]).astype(BF16)[0:ROWS]
        for n in range(WIDTH // 256):
            rows_n = jnp.dot(
                pick, rows_ref[:, n * 256:(n + 1) * 256], preferred_element_type=F32
            )
            for h in range(2):
                stage[pl.ds(g * ROWS * SUB + 2 * n + h, ROWS, stride=SUB), :] = rows_n[
                    :, h * 128:(h + 1) * 128
                ]

    def pack(row):
        return stage[tiles(row, SLOTS), :].astype(BF16).reshape(SLOTS, SUB, 128)

    def push(step, carry):
        block = pl.ds(step * SLOTS, SLOTS)
        send_buf[block] = pack(step * SLOTS)
        p = partner(step, sign)
        g = lax.div(step, GROUP)
        pltpu.make_async_remote_copy(
            src_ref=gate_send.at[pl.ds(step, 1)], dst_ref=gate_recv.at[pl.ds(step, 1)],
            send_sem=gate_send_sem, recv_sem=gate_recv_sem.at[g],
            device_id={"expert": p}, device_id_type=MESH,
        ).start()
        pltpu.make_async_remote_copy(
            src_ref=send_buf.at[block], dst_ref=recv_buf.at[block],
            send_sem=send_sem, recv_sem=recv_sem.at[g],
            device_id={"expert": p}, device_id_type=MESH,
        ).start()
        return carry

    gather(0)
    pl.semaphore_wait(barrier, PEERS + 2)
    lax.fori_loop(1, GROUP, push, 0)
    for g in range(1, GROUPS):
        gather(g)
        lax.fori_loop(g * GROUP, (g + 1) * GROUP, push, 0)
    recv_buf[0:SLOTS] = pack(0)
    gate_recv[0:1] = gate_send[0:1]

    own = iota((PEERS, CAP), 0) == me
    own_row = jnp.sum(jnp.where(own, chosen, 0), axis=0, keepdims=True)
    here, there = iota((CAP, CAP), 0), iota((CAP, CAP), 1)
    own_col = jnp.sum(jnp.where(here == there, own_row, 0), axis=1, keepdims=True)
    src_row, src_col = own_row >> 7, own_col >> 7
    loc_col = own_col & (TOK - 1)
    rank_col = jnp.sum(
        jnp.where((src_col == src_row) & (there < here), 1, 0), axis=1, keepdims=True
    )
    step_col = step_between(src_col, me)
    column_col = (step_col >> 4) * 128 + (step_col & (GROUP - 1)) * SLOTS + rank_col
    arrival = jnp.where(
        column_col == iota((CAP, GROUPS * 128), 1), 1.0, 0.0
    )
    onehot_loc = jnp.where(loc_col == iota((CAP, TOK), 1), 1.0, 0.0).astype(BF16)
    for g in range(GROUPS):
        block = slice(g * ROWS, (g + 1) * ROWS)
        place = jnp.transpose(arrival[:, g * 128:(g + 1) * 128]).astype(BF16)[0:ROWS]
        tok_of_row[block, :] = jnp.dot(place, onehot_loc, preferred_element_type=F32)
        for n in range(FF // 256):
            columns = slice(n * 256, (n + 1) * 256)
            act = jnp.dot(place, act_ref[:, columns], preferred_element_type=F32)
            hidden_n, slope_n = gelu_pair(act)
            hidden[block, columns] = hidden_n
            slope[block, columns] = slope_n
    for n in range(FF // 128):
        columns = slice(n * 128, (n + 1) * 128)
        hidden_t[columns, :] = jnp.transpose(hidden[:, columns]).astype(BF16)
    row_step = lax.div(iota((ROWS, GROUP), 0), SLOTS) == iota((ROWS, GROUP), 1)
    row_to_step = jnp.where(row_step, 1.0, 0.0).astype(BF16)

    def wait_bytes(source, target, sem, count):
        pltpu.make_async_copy(
            source.at[pl.ds(0, count)], target.at[pl.ds(0, count)], sem
        ).wait()

    def await_rows(g):
        steps = GROUP - 1 if g == 0 else GROUP
        wait_bytes(gate_send, gate_recv, gate_recv_sem.at[g], steps)
        wait_bytes(send_buf, recv_buf, recv_sem.at[g], steps * SLOTS)

    def unpack(source, g):
        for j in range(8):
            count = ROWS // 8
            stage[j * count * SUB:(j + 1) * count * SUB, :] = (
                source[g * ROWS + j * count:g * ROWS + (j + 1) * count]
                .astype(F32)
                .reshape(count * SUB, 128)
            )

    def arrive(g):
        block = slice(g * ROWS, (g + 1) * ROWS)
        unpack(recv_buf, g)
        gate_rows = jnp.dot(
            row_to_step,
            gate_recv[g * GROUP:(g + 1) * GROUP, 0, :].astype(BF16),
            preferred_element_type=F32,
        )
        gate_col = jnp.sum(gate_rows * tok_of_row[block, :], axis=1, keepdims=True)
        for c in range(SUB):
            columns = slice(c * 128, (c + 1) * 128)
            chunk = stage[pl.ds(c, ROWS, stride=SUB), :]
            rows2d[block, columns] = chunk.astype(BF16)
            scaled[block, columns] = (gate_col * chunk).astype(BF16)
        return gate_col

    def work(g, gate_col):
        block = slice(g * ROWS, (g + 1) * ROWS)
        gate_grad = jnp.zeros((ROWS, 1), F32)
        for n in range(FF // 256):
            columns = slice(n * 256, (n + 1) * 256)
            back = contract(rows2d[block, :], w_down[columns, :], 1, 1)
            gate_grad = gate_grad + jnp.sum(back * hidden[block, columns], axis=1, keepdims=True)
            pre_grad[:, columns] = (gate_col * back * slope[block, columns]).astype(BF16)
        marked = (gate_grad.astype(BF16).astype(F32) * tok_of_row[block, :]).astype(BF16)
        grad_send[g * GROUP:(g + 1) * GROUP, 0, :] = contract(row_to_step, marked, 0, 0)
        for n in range(WIDTH // 256):
            rows_n = contract(pre_grad[...], w_up[n * 256:(n + 1) * 256, :], 1, 1)
            for h in range(2):
                stage[pl.ds(2 * n + h, ROWS, stride=SUB), :] = rows_n[:, h * 128:(h + 1) * 128]
        for j in range(8):
            count = ROWS // 8
            back_buf[g * ROWS + j * count:g * ROWS + (j + 1) * count] = (
                stage[j * count * SUB:(j + 1) * count * SUB, :]
                .astype(BF16)
                .reshape(count, SUB, 128)
            )

    def push_back(step, carry):
        block = pl.ds(step * SLOTS, SLOTS)
        p = partner(step, -sign)
        g = lax.div(step, GROUP)
        pltpu.make_async_remote_copy(
            src_ref=grad_send.at[pl.ds(step, 1)], dst_ref=grad_recv.at[pl.ds(step, 1)],
            send_sem=grad_send_sem, recv_sem=grad_recv_sem.at[g],
            device_id={"expert": p}, device_id_type=MESH,
        ).start()
        pltpu.make_async_remote_copy(
            src_ref=back_buf.at[block], dst_ref=ret_buf.at[block],
            send_sem=back_send_sem, recv_sem=back_recv_sem.at[g],
            device_id={"expert": p}, device_id_type=MESH,
        ).start()
        return carry

    for g in range(GROUPS - 1):
        await_rows(g)
        gate_col = arrive(g)
        if g == 0:
            copy_down.wait()
            copy_up.wait()
        work(g, gate_col)
    lax.fori_loop(1, GROUP, push_back, 0)
    await_rows(GROUPS - 1)
    lax.fori_loop(GROUP, (GROUPS - 1) * GROUP, push_back, 0)
    gate_col = arrive(GROUPS - 1)

    for n in range(WIDTH // 256):
        columns = slice(n * 256, (n + 1) * 256)
        partial[:, columns] = jnp.dot(
            hidden_t[...], scaled[:, columns], preferred_element_type=F32
        ).astype(BF16)

    def pair_copy(b):
        return pltpu.make_async_remote_copy(
            src_ref=partial.at[pl.ds((2 * b + 1 - core) * BLOCK, BLOCK)],
            dst_ref=pair_recv.at[pl.ds(b * BLOCK, BLOCK)],
            send_sem=pair_send_sem, recv_sem=pair_recv_sem.at[b],
            device_id={"dp": sibling}, device_id_type=MESH,
        )

    for b in range(RING):
        pair_copy(b).start()
    work(GROUPS - 1, gate_col)
    lax.fori_loop((GROUPS - 1) * GROUP, PEERS, push_back, 0)
    ret_buf[0:SLOTS] = back_buf[0:SLOTS]
    grad_recv[0:1] = grad_send[0:1]

    for b in range(RING):
        pair_copy(b).wait_recv()
        both = pair_recv[b * BLOCK:(b + 1) * BLOCK, :].astype(F32) + partial[
            pl.ds((2 * b + core) * BLOCK, BLOCK), :
        ].astype(F32)
        pair_sum[b * BLOCK:(b + 1) * BLOCK, :] = both.astype(BF16)

    streams = ((0, 1, 4), (0, -1, 3), (1, 1, 3), (1, -1, 4))
    slot_of = {}
    for stream, (half, way, steps) in enumerate(streams):
        for s in range(1, steps + 1):
            slot_of[stream, s] = len(slot_of)

    def ring_copy(stream, s):
        half, way, steps = streams[stream]
        slot = slot_of[stream, s]
        block = lax.rem(my_x + way * (steps + 1 - s) + RING, RING)
        place = pl.ds(block * BLOCK + half * HALF, HALF)
        return place, slot, pltpu.make_async_remote_copy(
            src_ref=pair_sum.at[place] if s == 1 else ring_send.at[slot],
            dst_ref=ring_recv.at[slot],
            send_sem=ring_send_sem.at[slot], recv_sem=ring_recv_sem.at[slot],
            device_id={"dp": right if way == 1 else left}, device_id_type=MESH,
        )

    def ring_step(s):
        for stream, (half, way, steps) in enumerate(streams):
            if s > steps:
                continue
            place, slot, copy = ring_copy(stream, s)
            if s > 1:
                ring_copy(stream, s - 1)[2].wait_recv()
                total = ring_recv[slot_of[stream, s - 1]].astype(F32) + pair_sum[place, :].astype(F32)
                ring_send[slot] = total.astype(BF16)
            copy.start()

    def land(g):
        steps = GROUP - 1 if g == 0 else GROUP
        wait_bytes(grad_send, grad_recv, grad_recv_sem.at[g], steps)
        wait_bytes(back_buf, ret_buf, back_recv_sem.at[g], steps * SLOTS)
        unpack(ret_buf, g)
        for c in range(SUB):
            rows2d[g * ROWS:(g + 1) * ROWS, c * 128:(c + 1) * 128] = stage[
                pl.ds(c, ROWS, stride=SUB), :
            ].astype(BF16)

    ring_step(1)
    ring_step(2)
    land(0)
    ring_step(3)
    land(1)
    ring_step(4)
    for half in range(2):
        place = pl.ds(my_x * BLOCK + half * HALF, HALF)
        total = pair_sum[place, :].astype(F32)
        for stream, (of_half, way, steps) in enumerate(streams):
            if of_half == half:
                ring_copy(stream, steps)[2].wait_recv()
                total = total + ring_recv[slot_of[stream, steps]].astype(F32)
        down_out[half * HALF:(half + 1) * HALF, :] = total.astype(BF16)
    land(2)
    land(3)
    for n in range(WIDTH // 256):
        columns = slice(n * 256, (n + 1) * 256)
        total = jnp.zeros((TOK, 256), F32)
        for g in range(GROUPS):
            total = total + jnp.dot(
                landing[:, g * 128:g * 128 + ROWS],
                rows2d[g * ROWS:(g + 1) * ROWS, columns],
                preferred_element_type=F32,
            )
        tok_out[:, columns] = total.astype(BF16)
    gates = 1.0 / (1.0 + jnp.exp(-logits_ref[...]))
    step_to_expert = jnp.where(
        step_between(me, iota((PEERS, PEERS), 1)) == iota((PEERS, PEERS), 0), 1.0, 0.0
    ).astype(BF16)
    picked_grad = contract(grad_recv[:, 0, :].astype(BF16), step_to_expert, 0, 0)
    logit_out[...] = picked_grad * gates * (1.0 - gates)

    others = FLAT - SLOTS
    wait_bytes(send_buf, recv_buf, send_sem, others)
    wait_bytes(gate_send, gate_recv, gate_send_sem, PEERS - 1)
    wait_bytes(back_buf, ret_buf, back_send_sem, others)
    wait_bytes(grad_send, grad_recv, grad_send_sem, PEERS - 1)
    wait_bytes(pair_sum, pair_recv, pair_send_sem, RING * BLOCK)
    for stream, s in slot_of:
        ring_copy(stream, s)[2].wait_send()


def on_device(grad_out, router_logits, choices, pre_act, w_down, w_up):
    vmem = pl.BlockSpec(memory_space=pltpu.VMEM)
    anywhere = pl.BlockSpec(memory_space=pl.ANY)
    dma = pltpu.SemaphoreType.DMA
    tokens, logits, down = pl.pallas_call(
        kernel,
        out_shape=(
            jax.ShapeDtypeStruct((TOK, WIDTH), BF16),
            jax.ShapeDtypeStruct((TOK, PEERS), F32),
            jax.ShapeDtypeStruct((BLOCK, WIDTH), BF16),
        ),
        in_specs=[vmem, vmem, vmem, vmem, anywhere, anywhere],
        out_specs=(vmem, vmem, vmem),
        scratch_shapes=[
            pltpu.VMEM((FF, WIDTH), BF16),
            pltpu.VMEM((WIDTH, FF), BF16),
            pltpu.VMEM((FLAT * SUB, 128), F32),
            pltpu.VMEM((FLAT, SUB, 128), BF16),
            pltpu.VMEM((FLAT, SUB, 128), BF16),
            pltpu.VMEM((FLAT, SUB, 128), BF16),
            pltpu.VMEM((FLAT, SUB, 128), BF16),
            pltpu.VMEM((PEERS, 1, TOK), F32),
            pltpu.VMEM((PEERS, 1, TOK), F32),
            pltpu.VMEM((PEERS, 1, TOK), F32),
            pltpu.VMEM((PEERS, 1, TOK), F32),
            pltpu.VMEM((TOK, GROUPS * 128), BF16),
            pltpu.VMEM((FLAT, TOK), F32),
            pltpu.VMEM((FLAT, WIDTH), BF16),
            pltpu.VMEM((FLAT, WIDTH), BF16),
            pltpu.VMEM((FLAT, FF), F32),
            pltpu.VMEM((FLAT, FF), F32),
            pltpu.VMEM((FF, FLAT), BF16),
            pltpu.VMEM((ROWS, FF), BF16),
            pltpu.VMEM((FF, WIDTH), BF16),
            pltpu.VMEM((RING * BLOCK, WIDTH), BF16),
            pltpu.VMEM((RING * BLOCK, WIDTH), BF16),
            pltpu.VMEM((14, HALF, WIDTH), BF16),
            pltpu.VMEM((14, HALF, WIDTH), BF16),
            dma((2,)),
            dma, dma((GROUPS,)), dma, dma((GROUPS,)),
            dma, dma((GROUPS,)), dma, dma((GROUPS,)),
            dma, dma((RING,)), dma((14,)), dma((14,)),
        ],
        compiler_params=pltpu.CompilerParams(
            collective_id=0, has_side_effects=True, vmem_limit_bytes=56 << 20
        ),
        cost_estimate=pl.CostEstimate(
            flops=3 * 2 * CAP * FF * WIDTH, bytes_accessed=12 << 20, transcendentals=CAP * FF
        ),
        name="expert_backward",
    )(choices[0], router_logits[0], grad_out[0], pre_act[0, 0], w_down[0], w_up[0])
    return tokens[None], logits[None], down[None]


def solution(mesh):
    return jax.shard_map(
        on_device,
        mesh=mesh,
        in_specs=(
            P("dp", "expert", None),
            P("dp", "expert", None),
            P("dp", None, None),
            P("dp", "expert", None, None),
            P("expert", None, None),
            P("expert", None, None),
        ),
        out_specs=(P("dp", "expert", None), P("dp", "expert", None), P("expert", "dp", None)),
        check_vma=False,
    )
```

```python
import jax
import jax.numpy as jnp
from jax import lax
from jax.experimental import pallas as pl
from jax.experimental.pallas import tpu as pltpu
from jax.sharding import PartitionSpec as P

ROOT_TWO_PI = 0.7978845608028654
CUBIC = 0.044715
MESH = pl.DeviceIdType.MESH

SIDE = 8
PEERS = 64
RING = 8
TOK = 128
WIDTH = 2048
FF = 1024
CAP = 256
SLOTS = 6
FLAT = PEERS * SLOTS
SUB = 16
GROUP = 16
GROUPS = PEERS // GROUP
ROWS = GROUP * SLOTS
BLOCK = FF // (2 * RING)
HALF = BLOCK // 2

F32 = jnp.float32
BF16 = jnp.bfloat16
I32 = jnp.int32


def contract(left, right, left_dim, right_dim):
    return lax.dot_general(
        left, right, (((left_dim,), (right_dim,)), ((), ())), preferred_element_type=F32
    )


def gelu_pair(values):
    inner_arg = ROOT_TWO_PI * (values + CUBIC * values * values * values)
    tanh_part = jnp.tanh(inner_arg)
    hidden = 0.5 * values * (1.0 + tanh_part)
    slope_vals = 0.5 * (1.0 + tanh_part) + 0.5 * values * (
        1.0 - tanh_part * tanh_part
    ) * ROOT_TWO_PI * (1.0 + 3.0 * CUBIC * values * values)
    return hidden, slope_vals


def iota(shape, dim):
    return lax.broadcasted_iota(I32, shape, dim)


def kernel(
    choices_ref, logits_ref, rows_ref, act_ref, down_hbm, up_hbm,
    tok_out, logit_out, down_out,
    w_down, w_up, stage, send_buf, recv_buf, back_buf, ret_buf,
    gate_send, gate_recv, grad_send, grad_recv,
    landing, tok_of_row, rows2d, scaled, hidden, slope, hidden_t, pre_grad,
    partial, pair_recv, pair_sum, ring_send, ring_recv,
    weight_sem,
    send_sem, recv_sem, gate_send_sem, gate_recv_sem,
    back_send_sem, back_recv_sem, grad_send_sem, grad_recv_sem,
    pair_send_sem, pair_recv_sem, ring_send_sem, ring_recv_sem,
):
    me = lax.axis_index("expert")
    data = lax.axis_index("dp")
    my_z, my_y = lax.div(me, SIDE), lax.rem(me, SIDE)
    my_x, core = lax.div(data, 2), lax.rem(data, 2)
    sign = 1 - 2 * core

    def partner(step, way):
        dz = lax.rem(3 * step, SIDE)
        dy = lax.rem(2 * step + lax.div(step, SIDE), SIDE)
        z = lax.rem(my_z + way * dz + SIDE, SIDE)
        y = lax.rem(my_y + way * dy + SIDE, SIDE)
        return z * SIDE + y

    def step_between(origin, target):
        dz = jnp.bitwise_and(sign * ((target >> 3) - (origin >> 3)), SIDE - 1)
        dy = jnp.bitwise_and(sign * ((target & 7) - (origin & 7)), SIDE - 1)
        low = jnp.bitwise_and(3 * dz, SIDE - 1)
        return jnp.bitwise_and(dy - 2 * low, SIDE - 1) * SIDE + low

    right = lax.rem(my_x + 1, RING) * 2 + core
    left = lax.rem(my_x + RING - 1, RING) * 2 + core
    sibling = my_x * 2 + 1 - core

    copy_down = pltpu.make_async_copy(down_hbm, w_down, weight_sem.at[0])
    copy_up = pltpu.make_async_copy(up_hbm, w_up, weight_sem.at[1])
    copy_down.start()
    copy_up.start()

    barrier = pltpu.get_barrier_semaphore()

    def greet(step, carry):
        pl.semaphore_signal(
            barrier, inc=1, device_id={"expert": lax.rem(me + step, PEERS)}, device_id_type=MESH
        )
        return carry

    lax.fori_loop(1, PEERS, greet, 0)
    for other in (left, right, sibling):
        pl.semaphore_signal(barrier, inc=1, device_id={"dp": other}, device_id_type=MESH)

    chosen = choices_ref[...]
    mine = (chosen >> 7) == me
    token = jnp.where(mine, (chosen & (TOK - 1)) + 1, 0)
    lane = iota((PEERS, CAP), 1)
    before = jnp.where(mine, 1, 0)
    shift = 1
    while shift < CAP:
        before = before + jnp.where(lane >= shift, pltpu.roll(before, shift, 1), 0)
        shift *= 2
    column = iota((PEERS, GROUPS * 128), 1)
    within = column & 127
    step_in = (within * 43) >> 8
    slot_in = within - SLOTS * step_in
    at_step = step_between(me, iota((PEERS, GROUPS * 128), 0)) == (column >> 7) * GROUP + step_in
    at_step = at_step & (within < ROWS)
    spread = jnp.zeros((PEERS, GROUPS * 128), I32)
    for k in range(SLOTS):
        token_k = jnp.sum(jnp.where(before == k + 1, token, 0), axis=1, keepdims=True)
        spread = spread + jnp.where(at_step & (slot_in == k), token_k, 0)
    token_row = jnp.sum(spread, axis=0, keepdims=True) - 1
    landing_f = jnp.where(token_row == iota((TOK, GROUPS * 128), 0), 1.0, 0.0)
    landing[...] = landing_f.astype(BF16)

    expert_step = step_between(me, iota((PEERS, PEERS), 0)) == iota((PEERS, PEERS), 1)
    expert_to_step = jnp.where(expert_step, 1.0, 0.0).astype(BF16)
    gates = 1.0 / (1.0 + jnp.exp(-logits_ref[...]))
    gate_send[:, 0, :] = contract(expert_to_step, gates.astype(BF16), 0, 0)

    def tiles(row, count):
        return pl.ds(pl.multiple_of(row * SUB, SUB), count * SUB)

    def gather(g):
        pick = jnp.transpose(landing_f[:, g * 128:(g + 1) * 128]).astype(BF16)[0:ROWS]
        for n in range(WIDTH // 256):
            rows_n = jnp.dot(
                pick, rows_ref[:, n * 256:(n + 1) * 256], preferred_element_type=F32
            )
            for h in range(2):
                stage[pl.ds(g * ROWS * SUB + 2 * n + h, ROWS, stride=SUB), :] = rows_n[
                    :, h * 128:(h + 1) * 128
                ]

    def pack(row):
        return stage[tiles(row, SLOTS), :].astype(BF16).reshape(SLOTS, SUB, 128)

    def push(step, carry):
        block = pl.ds(step * SLOTS, SLOTS)
        send_buf[block] = pack(step * SLOTS)
        p = partner(step, sign)
        g = lax.div(step, GROUP)
        pltpu.make_async_remote_copy(
            src_ref=gate_send.at[pl.ds(step, 1)], dst_ref=gate_recv.at[pl.ds(step, 1)],
            send_sem=gate_send_sem, recv_sem=gate_recv_sem.at[g],
            device_id={"expert": p}, device_id_type=MESH,
        ).start()
        pltpu.make_async_remote_copy(
            src_ref=send_buf.at[block], dst_ref=recv_buf.at[block],
            send_sem=send_sem, recv_sem=recv_sem.at[g],
            device_id={"expert": p}, device_id_type=MESH,
        ).start()
        return carry

    gather(0)
    pl.semaphore_wait(barrier, PEERS + 2)
    lax.fori_loop(1, GROUP, push, 0)
    for g in range(1, GROUPS):
        gather(g)
        lax.fori_loop(g * GROUP, (g + 1) * GROUP, push, 0)
    recv_buf[0:SLOTS] = pack(0)
    gate_recv[0:1] = gate_send[0:1]

    own = iota((PEERS, CAP), 0) == me
    own_row = jnp.sum(jnp.where(own, chosen, 0), axis=0, keepdims=True)
    here, there = iota((CAP, CAP), 0), iota((CAP, CAP), 1)
    own_col = jnp.sum(jnp.where(here == there, own_row, 0), axis=1, keepdims=True)
    src_row, src_col = own_row >> 7, own_col >> 7
    loc_col = own_col & (TOK - 1)
    rank_col = jnp.sum(
        jnp.where((src_col == src_row) & (there < here), 1, 0), axis=1, keepdims=True
    )
    step_col = step_between(src_col, me)
    column_col = (step_col >> 4) * 128 + (step_col & (GROUP - 1)) * SLOTS + rank_col
    arrival = jnp.where(
        column_col == iota((CAP, GROUPS * 128), 1), 1.0, 0.0
    )
    onehot_loc = jnp.where(loc_col == iota((CAP, TOK), 1), 1.0, 0.0).astype(BF16)
    for g in range(GROUPS):
        block = slice(g * ROWS, (g + 1) * ROWS)
        place = jnp.transpose(arrival[:, g * 128:(g + 1) * 128]).astype(BF16)[0:ROWS]
        tok_of_row[block, :] = jnp.dot(place, onehot_loc, preferred_element_type=F32)
        for n in range(FF // 256):
            columns = slice(n * 256, (n + 1) * 256)
            act = jnp.dot(place, act_ref[:, columns], preferred_element_type=F32)
            hidden_n, slope_n = gelu_pair(act)
            hidden[block, columns] = hidden_n
            slope[block, columns] = slope_n
    for n in range(RING):
        turned = jnp.transpose(hidden[:, n * 128:(n + 1) * 128]).astype(BF16)
        hidden_t[pl.ds((1 - core) * (RING * BLOCK) + n * BLOCK, BLOCK), :] = turned[0:BLOCK]
        hidden_t[pl.ds(core * (RING * BLOCK) + n * BLOCK, BLOCK), :] = turned[BLOCK:]
    row_step = lax.div(iota((ROWS, GROUP), 0), SLOTS) == iota((ROWS, GROUP), 1)
    row_to_step = jnp.where(row_step, 1.0, 0.0).astype(BF16)

    def wait_bytes(source, target, sem, count):
        pltpu.make_async_copy(
            source.at[pl.ds(0, count)], target.at[pl.ds(0, count)], sem
        ).wait()

    def await_rows(g):
        steps = GROUP - 1 if g == 0 else GROUP
        wait_bytes(gate_send, gate_recv, gate_recv_sem.at[g], steps)
        wait_bytes(send_buf, recv_buf, recv_sem.at[g], steps * SLOTS)

    def unpack(source, g):
        for j in range(8):
            count = ROWS // 8
            stage[j * count * SUB:(j + 1) * count * SUB, :] = (
                source[g * ROWS + j * count:g * ROWS + (j + 1) * count]
                .astype(F32)
                .reshape(count * SUB, 128)
            )

    def arrive(g):
        block = slice(g * ROWS, (g + 1) * ROWS)
        unpack(recv_buf, g)
        gate_rows = jnp.dot(
            row_to_step,
            gate_recv[g * GROUP:(g + 1) * GROUP, 0, :].astype(BF16),
            preferred_element_type=F32,
        )
        gate_col = jnp.sum(gate_rows * tok_of_row[block, :], axis=1, keepdims=True)
        for c in range(SUB):
            columns = slice(c * 128, (c + 1) * 128)
            chunk = stage[pl.ds(c, ROWS, stride=SUB), :]
            rows2d[block, columns] = chunk.astype(BF16)
            scaled[block, columns] = (gate_col * chunk).astype(BF16)
        return gate_col

    def work(g, gate_col):
        block = slice(g * ROWS, (g + 1) * ROWS)
        gate_grad = jnp.zeros((ROWS, 1), F32)
        for n in range(FF // 256):
            columns = slice(n * 256, (n + 1) * 256)
            back = contract(rows2d[block, :], w_down[columns, :], 1, 1)
            gate_grad = gate_grad + jnp.sum(back * hidden[block, columns], axis=1, keepdims=True)
            pre_grad[:, columns] = (gate_col * back * slope[block, columns]).astype(BF16)
        marked = (gate_grad.astype(BF16).astype(F32) * tok_of_row[block, :]).astype(BF16)
        grad_send[g * GROUP:(g + 1) * GROUP, 0, :] = contract(row_to_step, marked, 0, 0)
        for n in range(WIDTH // 256):
            rows_n = contract(pre_grad[...], w_up[n * 256:(n + 1) * 256, :], 1, 1)
            for h in range(2):
                stage[pl.ds(2 * n + h, ROWS, stride=SUB), :] = rows_n[:, h * 128:(h + 1) * 128]
        for j in range(8):
            count = ROWS // 8
            back_buf[g * ROWS + j * count:g * ROWS + (j + 1) * count] = (
                stage[j * count * SUB:(j + 1) * count * SUB, :]
                .astype(BF16)
                .reshape(count, SUB, 128)
            )

    def push_back(step, carry):
        block = pl.ds(step * SLOTS, SLOTS)
        p = partner(step, -sign)
        g = lax.div(step, GROUP)
        pltpu.make_async_remote_copy(
            src_ref=grad_send.at[pl.ds(step, 1)], dst_ref=grad_recv.at[pl.ds(step, 1)],
            send_sem=grad_send_sem, recv_sem=grad_recv_sem.at[g],
            device_id={"expert": p}, device_id_type=MESH,
        ).start()
        pltpu.make_async_remote_copy(
            src_ref=back_buf.at[block], dst_ref=ret_buf.at[block],
            send_sem=back_send_sem, recv_sem=back_recv_sem.at[g],
            device_id={"expert": p}, device_id_type=MESH,
        ).start()
        return carry

    for g in range(GROUPS - 1):
        await_rows(g)
        gate_col = arrive(g)
        if g == 0:
            copy_down.wait()
            copy_up.wait()
        work(g, gate_col)
    lax.fori_loop(1, GROUP, push_back, 0)
    await_rows(GROUPS - 1)
    gate_col = arrive(GROUPS - 1)

    def multiply(half):
        rows = slice(half * RING * BLOCK, (half + 1) * RING * BLOCK)
        for n in range(WIDTH // 256):
            columns = slice(n * 256, (n + 1) * 256)
            partial[rows, columns] = jnp.dot(
                hidden_t[rows, :], scaled[:, columns], preferred_element_type=F32
            ).astype(BF16)

    away = (4, 3, -3, 2, -2, 1, -1, 0)

    def pair_copy(j):
        block = lax.rem(my_x + away[j] + RING, RING)
        return pltpu.make_async_remote_copy(
            src_ref=partial.at[pl.ds(block * BLOCK, BLOCK)],
            dst_ref=pair_recv.at[pl.ds(block * BLOCK, BLOCK)],
            send_sem=pair_send_sem, recv_sem=pair_recv_sem.at[j],
            device_id={"dp": sibling}, device_id_type=MESH,
        )

    def pair_add(j):
        pair_copy(j).wait_recv()
        block = lax.rem(my_x + away[j] + RING, RING)
        both = pair_recv[pl.ds(block * BLOCK, BLOCK), :].astype(F32) + partial[
            pl.ds((RING + block) * BLOCK, BLOCK), :
        ].astype(F32)
        pair_sum[pl.ds(block * BLOCK, BLOCK), :] = both.astype(BF16)

    multiply(0)
    for j in range(RING):
        pair_copy(j).start()
    multiply(1)
    lax.fori_loop(GROUP, (GROUPS - 1) * GROUP, push_back, 0)

    streams = ((0, 1, 4), (0, -1, 3), (1, 1, 3), (1, -1, 4))
    slot_of = {}
    for stream, (half, way, steps) in enumerate(streams):
        for s in range(1, steps + 1):
            slot_of[stream, s] = len(slot_of)

    def ring_copy(stream, s):
        half, way, steps = streams[stream]
        slot = slot_of[stream, s]
        block = lax.rem(my_x + way * (steps + 1 - s) + RING, RING)
        place = pl.ds(block * BLOCK + half * HALF, HALF)
        return place, slot, pltpu.make_async_remote_copy(
            src_ref=pair_sum.at[place] if s == 1 else ring_send.at[slot],
            dst_ref=ring_recv.at[slot],
            send_sem=ring_send_sem.at[slot], recv_sem=ring_recv_sem.at[slot],
            device_id={"dp": right if way == 1 else left}, device_id_type=MESH,
        )

    def ring_step(s):
        for stream, (half, way, steps) in enumerate(streams):
            if s > steps:
                continue
            place, slot, copy = ring_copy(stream, s)
            if s > 1:
                ring_copy(stream, s - 1)[2].wait_recv()
                total = ring_recv[slot_of[stream, s - 1]].astype(F32) + pair_sum[place, :].astype(F32)
                ring_send[slot] = total.astype(BF16)
            copy.start()

    def land(g):
        steps = GROUP - 1 if g == 0 else GROUP
        wait_bytes(grad_send, grad_recv, grad_recv_sem.at[g], steps)
        wait_bytes(back_buf, ret_buf, back_recv_sem.at[g], steps * SLOTS)
        unpack(ret_buf, g)
        for c in range(SUB):
            rows2d[g * ROWS:(g + 1) * ROWS, c * 128:(c + 1) * 128] = stage[
                pl.ds(c, ROWS, stride=SUB), :
            ].astype(BF16)

    for j in range(3):
        pair_add(j)
    ring_step(1)
    work(GROUPS - 1, gate_col)
    lax.fori_loop((GROUPS - 1) * GROUP, PEERS, push_back, 0)
    ret_buf[0:SLOTS] = back_buf[0:SLOTS]
    grad_recv[0:1] = grad_send[0:1]
    for j in range(3, RING):
        pair_add(j)
    ring_step(2)
    land(0)
    ring_step(3)
    land(1)
    ring_step(4)
    land(2)
    for half in range(2):
        place = pl.ds(my_x * BLOCK + half * HALF, HALF)
        total = pair_sum[place, :].astype(F32)
        for stream, (of_half, way, steps) in enumerate(streams):
            if of_half == half:
                ring_copy(stream, steps)[2].wait_recv()
                total = total + ring_recv[slot_of[stream, steps]].astype(F32)
        down_out[half * HALF:(half + 1) * HALF, :] = total.astype(BF16)
    land(3)
    for n in range(WIDTH // 256):
        columns = slice(n * 256, (n + 1) * 256)
        total = jnp.zeros((TOK, 256), F32)
        for g in range(GROUPS):
            total = total + jnp.dot(
                landing[:, g * 128:g * 128 + ROWS],
                rows2d[g * ROWS:(g + 1) * ROWS, columns],
                preferred_element_type=F32,
            )
        tok_out[:, columns] = total.astype(BF16)
    gates = 1.0 / (1.0 + jnp.exp(-logits_ref[...]))
    step_to_expert = jnp.where(
        step_between(me, iota((PEERS, PEERS), 1)) == iota((PEERS, PEERS), 0), 1.0, 0.0
    ).astype(BF16)
    picked_grad = contract(step_to_expert, grad_recv[:, 0, :].astype(BF16), 0, 0)
    logit_out[...] = picked_grad * gates * (1.0 - gates)

    others = FLAT - SLOTS
    wait_bytes(send_buf, recv_buf, send_sem, others)
    wait_bytes(gate_send, gate_recv, gate_send_sem, PEERS - 1)
    wait_bytes(back_buf, ret_buf, back_send_sem, others)
    wait_bytes(grad_send, grad_recv, grad_send_sem, PEERS - 1)
    wait_bytes(pair_sum, pair_recv, pair_send_sem, RING * BLOCK)
    for stream, s in slot_of:
        ring_copy(stream, s)[2].wait_send()


def hand_over(tokens, logits, down, tok_out, logit_out, down_out, sems):
    copies = [
        pltpu.make_async_copy(source, target, sems.at[i])
        for i, (source, target) in enumerate(
            ((tokens, tok_out), (logits, logit_out), (down, down_out))
        )
    ]
    for copy in copies:
        copy.start()
    for copy in copies:
        copy.wait()


def on_device(grad_out, router_logits, choices, pre_act, w_down, w_up):
    vmem = pl.BlockSpec(memory_space=pltpu.VMEM)
    anywhere = pl.BlockSpec(memory_space=pl.ANY)
    dma = pltpu.SemaphoreType.DMA
    tokens, logits, down = pl.pallas_call(
        kernel,
        out_shape=(
            jax.ShapeDtypeStruct((TOK, WIDTH), BF16),
            jax.ShapeDtypeStruct((PEERS, TOK), F32),
            jax.ShapeDtypeStruct((BLOCK, WIDTH), BF16),
        ),
        in_specs=[vmem, vmem, vmem, vmem, anywhere, anywhere],
        out_specs=(vmem, vmem, vmem),
        scratch_shapes=[
            pltpu.VMEM((FF, WIDTH), BF16),
            pltpu.VMEM((WIDTH, FF), BF16),
            pltpu.VMEM((FLAT * SUB, 128), F32),
            pltpu.VMEM((FLAT, SUB, 128), BF16),
            pltpu.VMEM((FLAT, SUB, 128), BF16),
            pltpu.VMEM((FLAT, SUB, 128), BF16),
            pltpu.VMEM((FLAT, SUB, 128), BF16),
            pltpu.VMEM((PEERS, 1, TOK), F32),
            pltpu.VMEM((PEERS, 1, TOK), F32),
            pltpu.VMEM((PEERS, 1, TOK), F32),
            pltpu.VMEM((PEERS, 1, TOK), F32),
            pltpu.VMEM((TOK, GROUPS * 128), BF16),
            pltpu.VMEM((FLAT, TOK), F32),
            pltpu.VMEM((FLAT, WIDTH), BF16),
            pltpu.VMEM((FLAT, WIDTH), BF16),
            pltpu.VMEM((FLAT, FF), F32),
            pltpu.VMEM((FLAT, FF), F32),
            pltpu.VMEM((FF, FLAT), BF16),
            pltpu.VMEM((ROWS, FF), BF16),
            pltpu.VMEM((FF, WIDTH), BF16),
            pltpu.VMEM((RING * BLOCK, WIDTH), BF16),
            pltpu.VMEM((RING * BLOCK, WIDTH), BF16),
            pltpu.VMEM((14, HALF, WIDTH), BF16),
            pltpu.VMEM((14, HALF, WIDTH), BF16),
            dma((2,)),
            dma, dma((GROUPS,)), dma, dma((GROUPS,)),
            dma, dma((GROUPS,)), dma, dma((GROUPS,)),
            dma, dma((RING,)), dma((14,)), dma((14,)),
        ],
        compiler_params=pltpu.CompilerParams(
            collective_id=0, has_side_effects=True, vmem_limit_bytes=56 << 20
        ),
        cost_estimate=pl.CostEstimate(
            flops=3 * 2 * CAP * FF * WIDTH, bytes_accessed=12 << 20, transcendentals=CAP * FF
        ),
        name="expert_backward",
    )(choices[0], router_logits[0].T, grad_out[0], pre_act[0, 0], w_down[0], w_up[0])
    tokens, logits, down = pl.pallas_call(
        hand_over,
        out_shape=[jax.ShapeDtypeStruct(x.shape, x.dtype) for x in (tokens, logits, down)],
        in_specs=[anywhere] * 3,
        out_specs=[anywhere] * 3,
        scratch_shapes=[dma((3,))],
        compiler_params=pltpu.CompilerParams(vmem_limit_bytes=60 << 20),
        name="hand_over",
    )(tokens, logits, down)
    return tokens[None], logits.T[None], down[None]


def solution(mesh):
    return jax.shard_map(
        on_device,
        mesh=mesh,
        in_specs=(
            P("dp", "expert", None),
            P("dp", "expert", None),
            P("dp", None, None),
            P("dp", "expert", None, None),
            P("expert", None, None),
            P("expert", None, None),
        ),
        out_specs=(P("dp", "expert", None), P("dp", "expert", None), P("expert", "dp", None)),
        check_vma=False,
    )
```

```python
import jax
import jax.numpy as jnp
from jax import lax
from jax.experimental import pallas as pl
from jax.experimental.pallas import tpu as pltpu
from jax.sharding import PartitionSpec as P

ROOT_TWO_PI = 0.7978845608028654
CUBIC = 0.044715
MESH = pl.DeviceIdType.MESH

SIDE = 8
PEERS = 64
RING = 8
TOK = 128
WIDTH = 2048
FF = 1024
CAP = 256
SLOTS = 6
FLAT = PEERS * SLOTS
SUB = 16
GROUP = 16
GROUPS = PEERS // GROUP
ROWS = GROUP * SLOTS
BLOCK = FF // (2 * RING)
HALF = BLOCK // 2

F32 = jnp.float32
BF16 = jnp.bfloat16
I32 = jnp.int32


def contract(left, right, left_dim, right_dim):
    return lax.dot_general(
        left, right, (((left_dim,), (right_dim,)), ((), ())), preferred_element_type=F32
    )


def gelu_pair(values):
    inner_arg = ROOT_TWO_PI * (values + CUBIC * values * values * values)
    tanh_part = jnp.tanh(inner_arg)
    hidden = 0.5 * values * (1.0 + tanh_part)
    slope_vals = 0.5 * (1.0 + tanh_part) + 0.5 * values * (
        1.0 - tanh_part * tanh_part
    ) * ROOT_TWO_PI * (1.0 + 3.0 * CUBIC * values * values)
    return hidden, slope_vals


def iota(shape, dim):
    return lax.broadcasted_iota(I32, shape, dim)


def kernel(
    choices_hbm, logits_hbm, rows_hbm, act_hbm, down_hbm, up_hbm,
    tok_out, logit_out, down_out,
    choices_ref, logits_ref, rows_ref, act_ref, w_down, w_up, tok_sum, stage, send_buf, recv_buf, back_buf, ret_buf,
    gate_send, gate_recv, grad_send, grad_recv,
    landing, tok_of_row, rows2d, scaled, hidden, slope, hidden_t, pre_grad,
    partial, pair_recv, pair_sum, ring_send, ring_recv,
    weight_sem,
    send_sem, recv_sem, gate_send_sem, gate_recv_sem,
    back_send_sem, back_recv_sem, grad_send_sem, grad_recv_sem,
    pair_send_sem, pair_recv_sem, ring_send_sem, ring_recv_sem,
):
    me = lax.axis_index("expert")
    data = lax.axis_index("dp")
    my_z, my_y = lax.div(me, SIDE), lax.rem(me, SIDE)
    my_x, core = lax.div(data, 2), lax.rem(data, 2)
    sign = 1 - 2 * core

    def partner(step, way):
        dz = lax.rem(3 * step, SIDE)
        dy = lax.rem(2 * step + lax.div(step, SIDE), SIDE)
        z = lax.rem(my_z + way * dz + SIDE, SIDE)
        y = lax.rem(my_y + way * dy + SIDE, SIDE)
        return z * SIDE + y

    def step_between(origin, target):
        dz = jnp.bitwise_and(sign * ((target >> 3) - (origin >> 3)), SIDE - 1)
        dy = jnp.bitwise_and(sign * ((target & 7) - (origin & 7)), SIDE - 1)
        low = jnp.bitwise_and(3 * dz, SIDE - 1)
        return jnp.bitwise_and(dy - 2 * low, SIDE - 1) * SIDE + low

    right = lax.rem(my_x + 1, RING) * 2 + core
    left = lax.rem(my_x + RING - 1, RING) * 2 + core
    sibling = my_x * 2 + 1 - core

    barrier = pltpu.get_barrier_semaphore()

    def greet(step, carry):
        pl.semaphore_signal(
            barrier, inc=1, device_id={"expert": lax.rem(me + step, PEERS)}, device_id_type=MESH
        )
        return carry

    lax.fori_loop(1, PEERS, greet, 0)
    for other in (left, right, sibling):
        pl.semaphore_signal(barrier, inc=1, device_id={"dp": other}, device_id_type=MESH)
    loads = [
        pltpu.make_async_copy(source, target, weight_sem.at[i])
        for i, (source, target) in enumerate(
            (
                (choices_hbm, choices_ref), (logits_hbm, logits_ref), (rows_hbm, rows_ref),
                (act_hbm, act_ref), (down_hbm, w_down), (up_hbm, w_up),
            )
        )
    ]
    for load in loads:
        load.start()
    loads[0].wait()

    chosen = choices_ref[...]
    mine = (chosen >> 7) == me
    token = jnp.where(mine, (chosen & (TOK - 1)) + 1, 0)
    lane = iota((PEERS, CAP), 1)
    before = jnp.where(mine, 1, 0)
    shift = 1
    while shift < CAP:
        before = before + jnp.where(lane >= shift, pltpu.roll(before, shift, 1), 0)
        shift *= 2
    column = iota((PEERS, GROUPS * 128), 1)
    within = column & 127
    step_in = (within * 43) >> 8
    slot_in = within - SLOTS * step_in
    at_step = step_between(me, iota((PEERS, GROUPS * 128), 0)) == (column >> 7) * GROUP + step_in
    at_step = at_step & (within < ROWS)
    spread = jnp.zeros((PEERS, GROUPS * 128), I32)
    for k in range(SLOTS):
        token_k = jnp.sum(jnp.where(before == k + 1, token, 0), axis=1, keepdims=True)
        spread = spread + jnp.where(at_step & (slot_in == k), token_k, 0)
    token_row = jnp.sum(spread, axis=0, keepdims=True) - 1
    landing_f = jnp.where(token_row == iota((TOK, GROUPS * 128), 0), 1.0, 0.0)
    landing[...] = landing_f.astype(BF16)

    expert_step = step_between(me, iota((PEERS, PEERS), 0)) == iota((PEERS, PEERS), 1)
    expert_to_step = jnp.where(expert_step, 1.0, 0.0).astype(BF16)
    loads[1].wait()
    gates = 1.0 / (1.0 + jnp.exp(-logits_ref[...]))
    gate_send[:, 0, :] = contract(expert_to_step, gates.astype(BF16), 0, 0)

    def tiles(row, count):
        return pl.ds(pl.multiple_of(row * SUB, SUB), count * SUB)

    def gather(g):
        pick = jnp.transpose(landing_f[:, g * 128:(g + 1) * 128]).astype(BF16)[0:ROWS]
        for n in range(WIDTH // 256):
            rows_n = jnp.dot(
                pick, rows_ref[:, n * 256:(n + 1) * 256], preferred_element_type=F32
            )
            for h in range(2):
                stage[pl.ds(g * ROWS * SUB + 2 * n + h, ROWS, stride=SUB), :] = rows_n[
                    :, h * 128:(h + 1) * 128
                ]

    def pack(row):
        return stage[tiles(row, SLOTS), :].astype(BF16).reshape(SLOTS, SUB, 128)

    def push(step, carry):
        block = pl.ds(step * SLOTS, SLOTS)
        send_buf[block] = pack(step * SLOTS)
        p = partner(step, sign)
        g = lax.div(step, GROUP)
        pltpu.make_async_remote_copy(
            src_ref=gate_send.at[pl.ds(step, 1)], dst_ref=gate_recv.at[pl.ds(step, 1)],
            send_sem=gate_send_sem, recv_sem=gate_recv_sem.at[g],
            device_id={"expert": p}, device_id_type=MESH,
        ).start()
        pltpu.make_async_remote_copy(
            src_ref=send_buf.at[block], dst_ref=recv_buf.at[block],
            send_sem=send_sem, recv_sem=recv_sem.at[g],
            device_id={"expert": p}, device_id_type=MESH,
        ).start()
        return carry

    loads[2].wait()
    gather(0)
    pl.semaphore_wait(barrier, PEERS + 2)
    lax.fori_loop(1, GROUP, push, 0)
    for g in range(1, GROUPS):
        gather(g)
        lax.fori_loop(g * GROUP, (g + 1) * GROUP, push, 0)
    recv_buf[0:SLOTS] = pack(0)
    gate_recv[0:1] = gate_send[0:1]

    own = iota((PEERS, CAP), 0) == me
    own_row = jnp.sum(jnp.where(own, chosen, 0), axis=0, keepdims=True)
    here, there = iota((CAP, CAP), 0), iota((CAP, CAP), 1)
    own_col = jnp.sum(jnp.where(here == there, own_row, 0), axis=1, keepdims=True)
    src_row, src_col = own_row >> 7, own_col >> 7
    loc_col = own_col & (TOK - 1)
    rank_col = jnp.sum(
        jnp.where((src_col == src_row) & (there < here), 1, 0), axis=1, keepdims=True
    )
    step_col = step_between(src_col, me)
    column_col = (step_col >> 4) * 128 + (step_col & (GROUP - 1)) * SLOTS + rank_col
    arrival = jnp.where(
        column_col == iota((CAP, GROUPS * 128), 1), 1.0, 0.0
    )
    onehot_loc = jnp.where(loc_col == iota((CAP, TOK), 1), 1.0, 0.0).astype(BF16)
    loads[3].wait()
    for g in range(GROUPS):
        block = slice(g * ROWS, (g + 1) * ROWS)
        place = jnp.transpose(arrival[:, g * 128:(g + 1) * 128]).astype(BF16)[0:ROWS]
        tok_of_row[block, :] = jnp.dot(place, onehot_loc, preferred_element_type=F32)
        for n in range(FF // 256):
            columns = slice(n * 256, (n + 1) * 256)
            act = jnp.dot(place, act_ref[:, columns], preferred_element_type=F32)
            hidden_n, slope_n = gelu_pair(act)
            hidden[block, columns] = hidden_n
            slope[block, columns] = slope_n
    for n in range(RING):
        turned = jnp.transpose(hidden[:, n * 128:(n + 1) * 128]).astype(BF16)
        hidden_t[pl.ds((1 - core) * (RING * BLOCK) + n * BLOCK, BLOCK), :] = turned[0:BLOCK]
        hidden_t[pl.ds(core * (RING * BLOCK) + n * BLOCK, BLOCK), :] = turned[BLOCK:]
    row_step = lax.div(iota((ROWS, GROUP), 0), SLOTS) == iota((ROWS, GROUP), 1)
    row_to_step = jnp.where(row_step, 1.0, 0.0).astype(BF16)

    def wait_bytes(source, target, sem, count):
        pltpu.make_async_copy(
            source.at[pl.ds(0, count)], target.at[pl.ds(0, count)], sem
        ).wait()

    def await_rows(g):
        steps = GROUP - 1 if g == 0 else GROUP
        wait_bytes(gate_send, gate_recv, gate_recv_sem.at[g], steps)
        wait_bytes(send_buf, recv_buf, recv_sem.at[g], steps * SLOTS)

    def unpack(source, g):
        for j in range(8):
            count = ROWS // 8
            stage[j * count * SUB:(j + 1) * count * SUB, :] = (
                source[g * ROWS + j * count:g * ROWS + (j + 1) * count]
                .astype(F32)
                .reshape(count * SUB, 128)
            )

    def arrive(g):
        block = slice(g * ROWS, (g + 1) * ROWS)
        unpack(recv_buf, g)
        gate_rows = jnp.dot(
            row_to_step,
            gate_recv[g * GROUP:(g + 1) * GROUP, 0, :].astype(BF16),
            preferred_element_type=F32,
        )
        gate_col = jnp.sum(gate_rows * tok_of_row[block, :], axis=1, keepdims=True)
        for c in range(SUB):
            columns = slice(c * 128, (c + 1) * 128)
            chunk = stage[pl.ds(c, ROWS, stride=SUB), :]
            rows2d[block, columns] = chunk.astype(BF16)
            scaled[block, columns] = (gate_col * chunk).astype(BF16)
        return gate_col

    def work(g, gate_col):
        block = slice(g * ROWS, (g + 1) * ROWS)
        gate_grad = jnp.zeros((ROWS, 1), F32)
        for n in range(FF // 256):
            columns = slice(n * 256, (n + 1) * 256)
            back = contract(rows2d[block, :], w_down[columns, :], 1, 1)
            gate_grad = gate_grad + jnp.sum(back * hidden[block, columns], axis=1, keepdims=True)
            pre_grad[:, columns] = (gate_col * back * slope[block, columns]).astype(BF16)
        marked = (gate_grad.astype(BF16).astype(F32) * tok_of_row[block, :]).astype(BF16)
        grad_send[g * GROUP:(g + 1) * GROUP, 0, :] = contract(row_to_step, marked, 0, 0)
        for n in range(WIDTH // 256):
            rows_n = contract(pre_grad[...], w_up[n * 256:(n + 1) * 256, :], 1, 1)
            for h in range(2):
                stage[pl.ds(2 * n + h, ROWS, stride=SUB), :] = rows_n[:, h * 128:(h + 1) * 128]
        for j in range(8):
            count = ROWS // 8
            back_buf[g * ROWS + j * count:g * ROWS + (j + 1) * count] = (
                stage[j * count * SUB:(j + 1) * count * SUB, :]
                .astype(BF16)
                .reshape(count, SUB, 128)
            )

    def push_back(step, carry):
        block = pl.ds(step * SLOTS, SLOTS)
        p = partner(step, -sign)
        g = lax.div(step, GROUP)
        pltpu.make_async_remote_copy(
            src_ref=grad_send.at[pl.ds(step, 1)], dst_ref=grad_recv.at[pl.ds(step, 1)],
            send_sem=grad_send_sem, recv_sem=grad_recv_sem.at[g],
            device_id={"expert": p}, device_id_type=MESH,
        ).start()
        pltpu.make_async_remote_copy(
            src_ref=back_buf.at[block], dst_ref=ret_buf.at[block],
            send_sem=back_send_sem, recv_sem=back_recv_sem.at[g],
            device_id={"expert": p}, device_id_type=MESH,
        ).start()
        return carry

    for g in range(GROUPS - 1):
        await_rows(g)
        gate_col = arrive(g)
        if g == 0:
            loads[4].wait()
            loads[5].wait()
        work(g, gate_col)
    lax.fori_loop(1, GROUP, push_back, 0)
    await_rows(GROUPS - 1)
    gate_col = arrive(GROUPS - 1)

    def multiply(half):
        rows = slice(half * RING * BLOCK, (half + 1) * RING * BLOCK)
        for n in range(WIDTH // 256):
            columns = slice(n * 256, (n + 1) * 256)
            partial[rows, columns] = jnp.dot(
                hidden_t[rows, :], scaled[:, columns], preferred_element_type=F32
            ).astype(BF16)

    away = (4, 3, -3, 2, -2, 1, -1, 0)

    def pair_copy(j):
        block = lax.rem(my_x + away[j] + RING, RING)
        return pltpu.make_async_remote_copy(
            src_ref=partial.at[pl.ds(block * BLOCK, BLOCK)],
            dst_ref=pair_recv.at[pl.ds(block * BLOCK, BLOCK)],
            send_sem=pair_send_sem, recv_sem=pair_recv_sem.at[j],
            device_id={"dp": sibling}, device_id_type=MESH,
        )

    def pair_add(j):
        pair_copy(j).wait_recv()
        block = lax.rem(my_x + away[j] + RING, RING)
        both = pair_recv[pl.ds(block * BLOCK, BLOCK), :].astype(F32) + partial[
            pl.ds((RING + block) * BLOCK, BLOCK), :
        ].astype(F32)
        pair_sum[pl.ds(block * BLOCK, BLOCK), :] = both.astype(BF16)

    multiply(0)
    for j in range(RING):
        pair_copy(j).start()
    multiply(1)
    lax.fori_loop(GROUP, (GROUPS - 1) * GROUP, push_back, 0)

    streams = ((0, 1, 4), (0, -1, 3), (1, 1, 3), (1, -1, 4))
    slot_of = {}
    for stream, (half, way, steps) in enumerate(streams):
        for s in range(1, steps + 1):
            slot_of[stream, s] = len(slot_of)

    def ring_copy(stream, s):
        half, way, steps = streams[stream]
        slot = slot_of[stream, s]
        block = lax.rem(my_x + way * (steps + 1 - s) + RING, RING)
        place = pl.ds(block * BLOCK + half * HALF, HALF)
        return place, slot, pltpu.make_async_remote_copy(
            src_ref=pair_sum.at[place] if s == 1 else ring_send.at[slot],
            dst_ref=ring_recv.at[slot],
            send_sem=ring_send_sem.at[slot], recv_sem=ring_recv_sem.at[slot],
            device_id={"dp": right if way == 1 else left}, device_id_type=MESH,
        )

    def ring_step(s):
        for stream, (half, way, steps) in enumerate(streams):
            if s > steps:
                continue
            place, slot, copy = ring_copy(stream, s)
            if s > 1:
                ring_copy(stream, s - 1)[2].wait_recv()
                total = ring_recv[slot_of[stream, s - 1]].astype(F32) + pair_sum[place, :].astype(F32)
                ring_send[slot] = total.astype(BF16)
            copy.start()

    def land(g):
        steps = GROUP - 1 if g == 0 else GROUP
        wait_bytes(grad_send, grad_recv, grad_recv_sem.at[g], steps)
        wait_bytes(back_buf, ret_buf, back_recv_sem.at[g], steps * SLOTS)
        unpack(ret_buf, g)
        for c in range(SUB):
            rows2d[g * ROWS:(g + 1) * ROWS, c * 128:(c + 1) * 128] = stage[
                pl.ds(c, ROWS, stride=SUB), :
            ].astype(BF16)

    for j in range(3):
        pair_add(j)
    ring_step(1)
    work(GROUPS - 1, gate_col)
    lax.fori_loop((GROUPS - 1) * GROUP, PEERS, push_back, 0)
    ret_buf[0:SLOTS] = back_buf[0:SLOTS]
    grad_recv[0:1] = grad_send[0:1]
    for j in range(3, RING):
        pair_add(j)
    ring_step(2)
    land(0)
    ring_step(3)
    land(1)
    ring_step(4)
    land(2)
    for half in range(2):
        place = pl.ds(my_x * BLOCK + half * HALF, HALF)
        total = pair_sum[place, :].astype(F32)
        for stream, (of_half, way, steps) in enumerate(streams):
            if of_half == half:
                ring_copy(stream, steps)[2].wait_recv()
                total = total + ring_recv[slot_of[stream, steps]].astype(F32)
        down_out[half * HALF:(half + 1) * HALF, :] = total.astype(BF16)
    def landed(g, columns):
        return jnp.dot(
            landing[:, g * 128:g * 128 + ROWS],
            rows2d[g * ROWS:(g + 1) * ROWS, columns],
            preferred_element_type=F32,
        )

    for n in range(WIDTH // 256):
        columns = slice(n * 256, (n + 1) * 256)
        tok_sum[:, columns] = landed(0, columns) + landed(1, columns) + landed(2, columns)
    land(3)
    for n in range(WIDTH // 256):
        columns = slice(n * 256, (n + 1) * 256)
        tok_out[:, columns] = (tok_sum[:, columns] + landed(3, columns)).astype(BF16)
    gates = 1.0 / (1.0 + jnp.exp(-logits_ref[...]))
    step_to_expert = jnp.where(
        step_between(me, iota((PEERS, PEERS), 1)) == iota((PEERS, PEERS), 0), 1.0, 0.0
    ).astype(BF16)
    picked_grad = contract(step_to_expert, grad_recv[:, 0, :].astype(BF16), 0, 0)
    logit_out[...] = picked_grad * gates * (1.0 - gates)

    others = FLAT - SLOTS
    wait_bytes(send_buf, recv_buf, send_sem, others)
    wait_bytes(gate_send, gate_recv, gate_send_sem, PEERS - 1)
    wait_bytes(back_buf, ret_buf, back_send_sem, others)
    wait_bytes(grad_send, grad_recv, grad_send_sem, PEERS - 1)
    wait_bytes(pair_sum, pair_recv, pair_send_sem, RING * BLOCK)
    for stream, s in slot_of:
        ring_copy(stream, s)[2].wait_send()


def hand_over(tokens, logits, down, tok_out, logit_out, down_out):
    tok_out[...] = tokens[...]
    logit_out[...] = logits[...]
    down_out[...] = down[...]


def on_device(grad_out, router_logits, choices, pre_act, w_down, w_up):
    vmem = pl.BlockSpec(memory_space=pltpu.VMEM)
    anywhere = pl.BlockSpec(memory_space=pl.ANY)
    dma = pltpu.SemaphoreType.DMA
    tokens, logits, down = pl.pallas_call(
        kernel,
        out_shape=(
            jax.ShapeDtypeStruct((TOK, WIDTH), BF16),
            jax.ShapeDtypeStruct((PEERS, TOK), F32),
            jax.ShapeDtypeStruct((BLOCK, WIDTH), BF16),
        ),
        in_specs=[anywhere] * 6,
        out_specs=(vmem, vmem, vmem),
        scratch_shapes=[
            pltpu.VMEM((PEERS, CAP), I32),
            pltpu.VMEM((PEERS, TOK), F32),
            pltpu.VMEM((TOK, WIDTH), BF16),
            pltpu.VMEM((CAP, FF), BF16),
            pltpu.VMEM((FF, WIDTH), BF16),
            pltpu.VMEM((WIDTH, FF), BF16),
            pltpu.VMEM((TOK, WIDTH), F32),
            pltpu.VMEM((FLAT * SUB, 128), F32),
            pltpu.VMEM((FLAT, SUB, 128), BF16),
            pltpu.VMEM((FLAT, SUB, 128), BF16),
            pltpu.VMEM((FLAT, SUB, 128), BF16),
            pltpu.VMEM((FLAT, SUB, 128), BF16),
            pltpu.VMEM((PEERS, 1, TOK), F32),
            pltpu.VMEM((PEERS, 1, TOK), F32),
            pltpu.VMEM((PEERS, 1, TOK), F32),
            pltpu.VMEM((PEERS, 1, TOK), F32),
            pltpu.VMEM((TOK, GROUPS * 128), BF16),
            pltpu.VMEM((FLAT, TOK), F32),
            pltpu.VMEM((FLAT, WIDTH), BF16),
            pltpu.VMEM((FLAT, WIDTH), BF16),
            pltpu.VMEM((FLAT, FF), F32),
            pltpu.VMEM((FLAT, FF), F32),
            pltpu.VMEM((FF, FLAT), BF16),
            pltpu.VMEM((ROWS, FF), BF16),
            pltpu.VMEM((FF, WIDTH), BF16),
            pltpu.VMEM((RING * BLOCK, WIDTH), BF16),
            pltpu.VMEM((RING * BLOCK, WIDTH), BF16),
            pltpu.VMEM((14, HALF, WIDTH), BF16),
            pltpu.VMEM((14, HALF, WIDTH), BF16),
            dma((6,)),
            dma, dma((GROUPS,)), dma, dma((GROUPS,)),
            dma, dma((GROUPS,)), dma, dma((GROUPS,)),
            dma, dma((RING,)), dma((14,)), dma((14,)),
        ],
        compiler_params=pltpu.CompilerParams(
            collective_id=0, has_side_effects=True, vmem_limit_bytes=60 << 20
        ),
        cost_estimate=pl.CostEstimate(
            flops=3 * 2 * CAP * FF * WIDTH, bytes_accessed=12 << 20, transcendentals=CAP * FF
        ),
        name="expert_backward",
    )(choices[0], router_logits[0].T, grad_out[0], pre_act[0, 0], w_down[0], w_up[0])
    tokens, logits, down = pl.pallas_call(
        hand_over,
        out_shape=[jax.ShapeDtypeStruct(x.shape, x.dtype) for x in (tokens, logits, down)],
        in_specs=[vmem] * 3,
        out_specs=[vmem] * 3,
        name="hand_over",
    )(tokens, logits, down)
    return tokens[None], logits.T[None], down[None]


def solution(mesh):
    return jax.shard_map(
        on_device,
        mesh=mesh,
        in_specs=(
            P("dp", "expert", None),
            P("dp", "expert", None),
            P("dp", None, None),
            P("dp", "expert", None, None),
            P("expert", None, None),
            P("expert", None, None),
        ),
        out_specs=(P("dp", "expert", None), P("dp", "expert", None), P("expert", "dp", None)),
        check_vma=False,
    )
```

```python
import jax
import jax.numpy as jnp
from jax import lax
from jax.experimental import pallas as pl
from jax.experimental.pallas import tpu as pltpu
from jax.sharding import PartitionSpec as P

ROOT_TWO_PI = 0.7978845608028654
CUBIC = 0.044715
MESH = pl.DeviceIdType.MESH

SIDE = 8
PEERS = 64
RING = 8
TOK = 128
WIDTH = 2048
FF = 1024
CAP = 256
SLOTS = 6
FLAT = PEERS * SLOTS
SUB = 16
GROUP = 16
GROUPS = PEERS // GROUP
ROWS = GROUP * SLOTS
BLOCK = FF // (2 * RING)
HALF = BLOCK // 2

F32 = jnp.float32
BF16 = jnp.bfloat16
I32 = jnp.int32


def contract(left, right, left_dim, right_dim):
    return lax.dot_general(
        left, right, (((left_dim,), (right_dim,)), ((), ())), preferred_element_type=F32
    )


def gelu_pair(values):
    inner_arg = ROOT_TWO_PI * (values + CUBIC * values * values * values)
    tanh_part = jnp.tanh(inner_arg)
    hidden = 0.5 * values * (1.0 + tanh_part)
    slope_vals = 0.5 * (1.0 + tanh_part) + 0.5 * values * (
        1.0 - tanh_part * tanh_part
    ) * ROOT_TWO_PI * (1.0 + 3.0 * CUBIC * values * values)
    return hidden, slope_vals


def iota(shape, dim):
    return lax.broadcasted_iota(I32, shape, dim)


def kernel(
    choices_hbm, logits_hbm, rows_hbm, act_hbm, down_hbm, up_hbm,
    tok_out, logit_out, down_out,
    choices_ref, logits_ref, rows_ref, act_ref, w_down, w_up, tok_sum, stage, send_buf, recv_buf, back_buf, ret_buf,
    gate_send, gate_recv, grad_send, grad_recv,
    landing, tok_of_row, rows2d, scaled, hidden, slope, hidden_t, pre_grad,
    partial, pair_recv, pair_sum, ring_send, ring_recv,
    weight_sem,
    send_sem, recv_sem, gate_send_sem, gate_recv_sem,
    back_send_sem, back_recv_sem, grad_send_sem, grad_recv_sem,
    pair_send_sem, pair_recv_sem, ring_send_sem, ring_recv_sem,
):
    me = lax.axis_index("expert")
    data = lax.axis_index("dp")
    my_z, my_y = lax.div(me, SIDE), lax.rem(me, SIDE)
    my_x, core = lax.div(data, 2), lax.rem(data, 2)
    sign = 1 - 2 * core

    def partner(step, way):
        dz = lax.rem(3 * step, SIDE)
        dy = lax.rem(2 * step + lax.div(step, SIDE), SIDE)
        z = lax.rem(my_z + way * dz + SIDE, SIDE)
        y = lax.rem(my_y + way * dy + SIDE, SIDE)
        return z * SIDE + y

    def step_between(origin, target):
        dz = jnp.bitwise_and(sign * ((target >> 3) - (origin >> 3)), SIDE - 1)
        dy = jnp.bitwise_and(sign * ((target & 7) - (origin & 7)), SIDE - 1)
        low = jnp.bitwise_and(3 * dz, SIDE - 1)
        return jnp.bitwise_and(dy - 2 * low, SIDE - 1) * SIDE + low

    right = lax.rem(my_x + 1, RING) * 2 + core
    left = lax.rem(my_x + RING - 1, RING) * 2 + core
    sibling = my_x * 2 + 1 - core

    barrier = pltpu.get_barrier_semaphore()

    def greet(step, carry):
        pl.semaphore_signal(
            barrier, inc=1, device_id={"expert": lax.rem(me + step, PEERS)}, device_id_type=MESH
        )
        return carry

    lax.fori_loop(1, PEERS, greet, 0)
    for other in (left, right, sibling):
        pl.semaphore_signal(barrier, inc=1, device_id={"dp": other}, device_id_type=MESH)
    loads = [
        pltpu.make_async_copy(source, target, weight_sem.at[i])
        for i, (source, target) in enumerate(
            (
                (choices_hbm, choices_ref), (logits_hbm, logits_ref), (rows_hbm, rows_ref),
                (act_hbm, act_ref), (down_hbm, w_down), (up_hbm, w_up),
            )
        )
    ]
    for load in loads:
        load.start()
    loads[0].wait()

    chosen = choices_ref[...]
    mine = (chosen >> 7) == me
    token = jnp.where(mine, (chosen & (TOK - 1)) + 1, 0)
    lane = iota((PEERS, CAP), 1)
    before = jnp.where(mine, 1, 0)
    shift = 1
    while shift < CAP:
        before = before + jnp.where(lane >= shift, pltpu.roll(before, shift, 1), 0)
        shift *= 2
    column = iota((PEERS, GROUPS * 128), 1)
    within = column & 127
    step_in = (within * 43) >> 8
    slot_in = within - SLOTS * step_in
    at_step = step_between(me, iota((PEERS, GROUPS * 128), 0)) == (column >> 7) * GROUP + step_in
    at_step = at_step & (within < ROWS)
    spread = jnp.zeros((PEERS, GROUPS * 128), I32)
    for k in range(SLOTS):
        token_k = jnp.sum(jnp.where(before == k + 1, token, 0), axis=1, keepdims=True)
        spread = spread + jnp.where(at_step & (slot_in == k), token_k, 0)
    token_row = jnp.sum(spread, axis=0, keepdims=True) - 1
    landing_f = jnp.where(token_row == iota((TOK, GROUPS * 128), 0), 1.0, 0.0)
    landing[...] = landing_f.astype(BF16)

    expert_step = step_between(me, iota((PEERS, PEERS), 0)) == iota((PEERS, PEERS), 1)
    expert_to_step = jnp.where(expert_step, 1.0, 0.0).astype(BF16)
    loads[1].wait()
    gates = 1.0 / (1.0 + jnp.exp(-logits_ref[...]))
    gate_send[:, 0, :] = contract(expert_to_step, gates.astype(BF16), 0, 0)

    def tiles(row, count):
        return pl.ds(pl.multiple_of(row * SUB, SUB), count * SUB)

    def gather(g):
        pick = jnp.transpose(landing_f[:, g * 128:(g + 1) * 128]).astype(BF16)[0:ROWS]
        for n in range(WIDTH // 256):
            rows_n = jnp.dot(
                pick, rows_ref[:, n * 256:(n + 1) * 256], preferred_element_type=F32
            )
            for h in range(2):
                stage[pl.ds(g * ROWS * SUB + 2 * n + h, ROWS, stride=SUB), :] = rows_n[
                    :, h * 128:(h + 1) * 128
                ]

    def pack(row):
        return stage[tiles(row, SLOTS), :].astype(BF16).reshape(SLOTS, SUB, 128)

    def push(step, carry):
        block = pl.ds(step * SLOTS, SLOTS)
        send_buf[block] = pack(step * SLOTS)
        p = partner(step, sign)
        g = lax.div(step, GROUP)
        pltpu.make_async_remote_copy(
            src_ref=gate_send.at[pl.ds(step, 1)], dst_ref=gate_recv.at[pl.ds(step, 1)],
            send_sem=gate_send_sem, recv_sem=gate_recv_sem.at[g],
            device_id={"expert": p}, device_id_type=MESH,
        ).start()
        pltpu.make_async_remote_copy(
            src_ref=send_buf.at[block], dst_ref=recv_buf.at[block],
            send_sem=send_sem, recv_sem=recv_sem.at[g],
            device_id={"expert": p}, device_id_type=MESH,
        ).start()
        return carry

    loads[2].wait()
    gather(0)
    pl.semaphore_wait(barrier, PEERS + 2)
    lax.fori_loop(1, GROUP, push, 0)
    for g in range(1, GROUPS):
        gather(g)
        lax.fori_loop(g * GROUP, (g + 1) * GROUP, push, 0)
    recv_buf[0:SLOTS] = pack(0)
    gate_recv[0:1] = gate_send[0:1]

    own = iota((PEERS, CAP), 0) == me
    own_row = jnp.sum(jnp.where(own, chosen, 0), axis=0, keepdims=True)
    here, there = iota((CAP, CAP), 0), iota((CAP, CAP), 1)
    own_col = jnp.sum(jnp.where(here == there, own_row, 0), axis=1, keepdims=True)
    src_row, src_col = own_row >> 7, own_col >> 7
    loc_col = own_col & (TOK - 1)
    rank_col = jnp.sum(
        jnp.where((src_col == src_row) & (there < here), 1, 0), axis=1, keepdims=True
    )
    step_col = step_between(src_col, me)
    column_col = (step_col >> 4) * 128 + (step_col & (GROUP - 1)) * SLOTS + rank_col
    arrival = jnp.where(
        column_col == iota((CAP, GROUPS * 128), 1), 1.0, 0.0
    )
    onehot_loc = jnp.where(loc_col == iota((CAP, TOK), 1), 1.0, 0.0).astype(BF16)
    loads[3].wait()
    for g in range(GROUPS):
        block = slice(g * ROWS, (g + 1) * ROWS)
        place = jnp.transpose(arrival[:, g * 128:(g + 1) * 128]).astype(BF16)[0:ROWS]
        tok_of_row[block, :] = jnp.dot(place, onehot_loc, preferred_element_type=F32)
        for n in range(FF // 256):
            columns = slice(n * 256, (n + 1) * 256)
            act = jnp.dot(place, act_ref[:, columns], preferred_element_type=F32)
            hidden_n, slope_n = gelu_pair(act)
            hidden[block, columns] = hidden_n
            slope[block, columns] = slope_n
    for n in range(RING):
        turned = jnp.transpose(hidden[:, n * 128:(n + 1) * 128]).astype(BF16)
        hidden_t[pl.ds((1 - core) * (RING * BLOCK) + n * BLOCK, BLOCK), :] = turned[0:BLOCK]
        hidden_t[pl.ds(core * (RING * BLOCK) + n * BLOCK, BLOCK), :] = turned[BLOCK:]
    row_step = lax.div(iota((ROWS, GROUP), 0), SLOTS) == iota((ROWS, GROUP), 1)
    row_to_step = jnp.where(row_step, 1.0, 0.0).astype(BF16)

    def wait_bytes(source, target, sem, count):
        pltpu.make_async_copy(
            source.at[pl.ds(0, count)], target.at[pl.ds(0, count)], sem
        ).wait()

    def await_rows(g):
        steps = GROUP - 1 if g == 0 else GROUP
        wait_bytes(gate_send, gate_recv, gate_recv_sem.at[g], steps)
        wait_bytes(send_buf, recv_buf, recv_sem.at[g], steps * SLOTS)

    def unpack(source, g):
        for j in range(8):
            count = ROWS // 8
            stage[j * count * SUB:(j + 1) * count * SUB, :] = (
                source[g * ROWS + j * count:g * ROWS + (j + 1) * count]
                .astype(F32)
                .reshape(count * SUB, 128)
            )

    def arrive(g):
        block = slice(g * ROWS, (g + 1) * ROWS)
        unpack(recv_buf, g)
        gate_rows = jnp.dot(
            row_to_step,
            gate_recv[g * GROUP:(g + 1) * GROUP, 0, :].astype(BF16),
            preferred_element_type=F32,
        )
        gate_col = jnp.sum(gate_rows * tok_of_row[block, :], axis=1, keepdims=True)
        for c in range(SUB):
            columns = slice(c * 128, (c + 1) * 128)
            chunk = stage[pl.ds(c, ROWS, stride=SUB), :]
            rows2d[block, columns] = chunk.astype(BF16)
            scaled[block, columns] = (gate_col * chunk).astype(BF16)
        return gate_col

    def work(g, gate_col):
        block = slice(g * ROWS, (g + 1) * ROWS)
        gate_grad = jnp.zeros((ROWS, 1), F32)
        for n in range(FF // 256):
            columns = slice(n * 256, (n + 1) * 256)
            back = contract(rows2d[block, :], w_down[columns, :], 1, 1)
            gate_grad = gate_grad + jnp.sum(back * hidden[block, columns], axis=1, keepdims=True)
            pre_grad[:, columns] = (gate_col * back * slope[block, columns]).astype(BF16)
        marked = (gate_grad.astype(BF16).astype(F32) * tok_of_row[block, :]).astype(BF16)
        grad_send[g * GROUP:(g + 1) * GROUP, 0, :] = contract(row_to_step, marked, 0, 0)
        for n in range(WIDTH // 256):
            rows_n = contract(pre_grad[...], w_up[n * 256:(n + 1) * 256, :], 1, 1)
            for h in range(2):
                stage[pl.ds(2 * n + h, ROWS, stride=SUB), :] = rows_n[:, h * 128:(h + 1) * 128]
        for j in range(8):
            count = ROWS // 8
            back_buf[g * ROWS + j * count:g * ROWS + (j + 1) * count] = (
                stage[j * count * SUB:(j + 1) * count * SUB, :]
                .astype(BF16)
                .reshape(count, SUB, 128)
            )

    def push_back(step, carry):
        block = pl.ds(step * SLOTS, SLOTS)
        p = partner(step, -sign)
        g = lax.div(step, GROUP)
        pltpu.make_async_remote_copy(
            src_ref=grad_send.at[pl.ds(step, 1)], dst_ref=grad_recv.at[pl.ds(step, 1)],
            send_sem=grad_send_sem, recv_sem=grad_recv_sem.at[g],
            device_id={"expert": p}, device_id_type=MESH,
        ).start()
        pltpu.make_async_remote_copy(
            src_ref=back_buf.at[block], dst_ref=ret_buf.at[block],
            send_sem=back_send_sem, recv_sem=back_recv_sem.at[g],
            device_id={"expert": p}, device_id_type=MESH,
        ).start()
        return carry

    for g in range(GROUPS - 1):
        await_rows(g)
        gate_col = arrive(g)
        if g == 0:
            loads[4].wait()
            loads[5].wait()
        work(g, gate_col)
        if g > 0:
            lax.fori_loop(max(1, (g - 1) * GROUP), g * GROUP, push_back, 0)
    await_rows(GROUPS - 1)
    gate_col = arrive(GROUPS - 1)

    def multiply(half):
        rows = slice(half * RING * BLOCK, (half + 1) * RING * BLOCK)
        for n in range(WIDTH // 256):
            columns = slice(n * 256, (n + 1) * 256)
            partial[rows, columns] = jnp.dot(
                hidden_t[rows, :], scaled[:, columns], preferred_element_type=F32
            ).astype(BF16)

    away = (4, 3, -3, 2, -2, 1, -1, 0)

    def pair_copy(j):
        block = lax.rem(my_x + away[j] + RING, RING)
        return pltpu.make_async_remote_copy(
            src_ref=partial.at[pl.ds(block * BLOCK, BLOCK)],
            dst_ref=pair_recv.at[pl.ds(block * BLOCK, BLOCK)],
            send_sem=pair_send_sem, recv_sem=pair_recv_sem.at[j],
            device_id={"dp": sibling}, device_id_type=MESH,
        )

    def pair_add(j):
        pair_copy(j).wait_recv()
        block = lax.rem(my_x + away[j] + RING, RING)
        both = pair_recv[pl.ds(block * BLOCK, BLOCK), :].astype(F32) + partial[
            pl.ds((RING + block) * BLOCK, BLOCK), :
        ].astype(F32)
        pair_sum[pl.ds(block * BLOCK, BLOCK), :] = both.astype(BF16)

    multiply(0)
    for j in range(RING):
        pair_copy(j).start()
    lax.fori_loop((GROUPS - 2) * GROUP, (GROUPS - 1) * GROUP, push_back, 0)
    multiply(1)

    streams = ((0, 1, 4), (0, -1, 3), (1, 1, 3), (1, -1, 4))
    slot_of = {}
    for stream, (half, way, steps) in enumerate(streams):
        for s in range(1, steps + 1):
            slot_of[stream, s] = len(slot_of)

    def ring_copy(stream, s):
        half, way, steps = streams[stream]
        slot = slot_of[stream, s]
        block = lax.rem(my_x + way * (steps + 1 - s) + RING, RING)
        place = pl.ds(block * BLOCK + half * HALF, HALF)
        return place, slot, pltpu.make_async_remote_copy(
            src_ref=pair_sum.at[place] if s == 1 else ring_send.at[slot],
            dst_ref=ring_recv.at[slot],
            send_sem=ring_send_sem.at[slot], recv_sem=ring_recv_sem.at[slot],
            device_id={"dp": right if way == 1 else left}, device_id_type=MESH,
        )

    def ring_step(s):
        for stream, (half, way, steps) in enumerate(streams):
            if s > steps:
                continue
            place, slot, copy = ring_copy(stream, s)
            if s > 1:
                ring_copy(stream, s - 1)[2].wait_recv()
                total = ring_recv[slot_of[stream, s - 1]].astype(F32) + pair_sum[place, :].astype(F32)
                ring_send[slot] = total.astype(BF16)
            copy.start()

    def land(g):
        steps = GROUP - 1 if g == 0 else GROUP
        wait_bytes(grad_send, grad_recv, grad_recv_sem.at[g], steps)
        wait_bytes(back_buf, ret_buf, back_recv_sem.at[g], steps * SLOTS)
        unpack(ret_buf, g)
        for c in range(SUB):
            rows2d[g * ROWS:(g + 1) * ROWS, c * 128:(c + 1) * 128] = stage[
                pl.ds(c, ROWS, stride=SUB), :
            ].astype(BF16)

    for j in range(3):
        pair_add(j)
    ring_step(1)
    work(GROUPS - 1, gate_col)
    lax.fori_loop((GROUPS - 1) * GROUP, PEERS, push_back, 0)
    ret_buf[0:SLOTS] = back_buf[0:SLOTS]
    grad_recv[0:1] = grad_send[0:1]
    for j in range(3, RING):
        pair_add(j)
    ring_step(2)
    land(0)
    ring_step(3)
    land(1)
    ring_step(4)
    land(2)
    for half in range(2):
        place = pl.ds(my_x * BLOCK + half * HALF, HALF)
        total = pair_sum[place, :].astype(F32)
        for stream, (of_half, way, steps) in enumerate(streams):
            if of_half == half:
                ring_copy(stream, steps)[2].wait_recv()
                total = total + ring_recv[slot_of[stream, steps]].astype(F32)
        down_out[half * HALF:(half + 1) * HALF, :] = total.astype(BF16)
    def landed(g, columns):
        return jnp.dot(
            landing[:, g * 128:g * 128 + ROWS],
            rows2d[g * ROWS:(g + 1) * ROWS, columns],
            preferred_element_type=F32,
        )

    for n in range(WIDTH // 256):
        columns = slice(n * 256, (n + 1) * 256)
        tok_sum[:, columns] = landed(0, columns) + landed(1, columns) + landed(2, columns)
    land(3)
    for n in range(WIDTH // 256):
        columns = slice(n * 256, (n + 1) * 256)
        tok_out[:, columns] = (tok_sum[:, columns] + landed(3, columns)).astype(BF16)
    gates = 1.0 / (1.0 + jnp.exp(-logits_ref[...]))
    step_to_expert = jnp.where(
        step_between(me, iota((PEERS, PEERS), 1)) == iota((PEERS, PEERS), 0), 1.0, 0.0
    ).astype(BF16)
    picked_grad = contract(step_to_expert, grad_recv[:, 0, :].astype(BF16), 0, 0)
    logit_out[...] = picked_grad * gates * (1.0 - gates)

    others = FLAT - SLOTS
    wait_bytes(send_buf, recv_buf, send_sem, others)
    wait_bytes(gate_send, gate_recv, gate_send_sem, PEERS - 1)
    wait_bytes(back_buf, ret_buf, back_send_sem, others)
    wait_bytes(grad_send, grad_recv, grad_send_sem, PEERS - 1)
    wait_bytes(pair_sum, pair_recv, pair_send_sem, RING * BLOCK)
    for stream, s in slot_of:
        ring_copy(stream, s)[2].wait_send()


def hand_over(tokens, logits, down, tok_out, logit_out, down_out):
    tok_out[...] = tokens[...]
    logit_out[...] = logits[...]
    down_out[...] = down[...]


def on_device(grad_out, router_logits, choices, pre_act, w_down, w_up):
    vmem = pl.BlockSpec(memory_space=pltpu.VMEM)
    anywhere = pl.BlockSpec(memory_space=pl.ANY)
    dma = pltpu.SemaphoreType.DMA
    tokens, logits, down = pl.pallas_call(
        kernel,
        out_shape=(
            jax.ShapeDtypeStruct((TOK, WIDTH), BF16),
            jax.ShapeDtypeStruct((PEERS, TOK), F32),
            jax.ShapeDtypeStruct((BLOCK, WIDTH), BF16),
        ),
        in_specs=[anywhere] * 6,
        out_specs=(vmem, vmem, vmem),
        scratch_shapes=[
            pltpu.VMEM((PEERS, CAP), I32),
            pltpu.VMEM((PEERS, TOK), F32),
            pltpu.VMEM((TOK, WIDTH), BF16),
            pltpu.VMEM((CAP, FF), BF16),
            pltpu.VMEM((FF, WIDTH), BF16),
            pltpu.VMEM((WIDTH, FF), BF16),
            pltpu.VMEM((TOK, WIDTH), F32),
            pltpu.VMEM((FLAT * SUB, 128), F32),
            pltpu.VMEM((FLAT, SUB, 128), BF16),
            pltpu.VMEM((FLAT, SUB, 128), BF16),
            pltpu.VMEM((FLAT, SUB, 128), BF16),
            pltpu.VMEM((FLAT, SUB, 128), BF16),
            pltpu.VMEM((PEERS, 1, TOK), F32),
            pltpu.VMEM((PEERS, 1, TOK), F32),
            pltpu.VMEM((PEERS, 1, TOK), F32),
            pltpu.VMEM((PEERS, 1, TOK), F32),
            pltpu.VMEM((TOK, GROUPS * 128), BF16),
            pltpu.VMEM((FLAT, TOK), F32),
            pltpu.VMEM((FLAT, WIDTH), BF16),
            pltpu.VMEM((FLAT, WIDTH), BF16),
            pltpu.VMEM((FLAT, FF), F32),
            pltpu.VMEM((FLAT, FF), F32),
            pltpu.VMEM((FF, FLAT), BF16),
            pltpu.VMEM((ROWS, FF), BF16),
            pltpu.VMEM((FF, WIDTH), BF16),
            pltpu.VMEM((RING * BLOCK, WIDTH), BF16),
            pltpu.VMEM((RING * BLOCK, WIDTH), BF16),
            pltpu.VMEM((14, HALF, WIDTH), BF16),
            pltpu.VMEM((14, HALF, WIDTH), BF16),
            dma((6,)),
            dma, dma((GROUPS,)), dma, dma((GROUPS,)),
            dma, dma((GROUPS,)), dma, dma((GROUPS,)),
            dma, dma((RING,)), dma((14,)), dma((14,)),
        ],
        compiler_params=pltpu.CompilerParams(
            collective_id=0, has_side_effects=True, vmem_limit_bytes=60 << 20
        ),
        cost_estimate=pl.CostEstimate(
            flops=3 * 2 * CAP * FF * WIDTH, bytes_accessed=12 << 20, transcendentals=CAP * FF
        ),
        name="expert_backward",
    )(choices[0], router_logits[0].T, grad_out[0], pre_act[0, 0], w_down[0], w_up[0])
    tokens, logits, down = pl.pallas_call(
        hand_over,
        out_shape=[jax.ShapeDtypeStruct(x.shape, x.dtype) for x in (tokens, logits, down)],
        in_specs=[vmem] * 3,
        out_specs=[vmem] * 3,
        name="hand_over",
    )(tokens, logits, down)
    return tokens[None], logits.T[None], down[None]


def solution(mesh):
    return jax.shard_map(
        on_device,
        mesh=mesh,
        in_specs=(
            P("dp", "expert", None),
            P("dp", "expert", None),
            P("dp", None, None),
            P("dp", "expert", None, None),
            P("expert", None, None),
            P("expert", None, None),
        ),
        out_specs=(P("dp", "expert", None), P("dp", "expert", None), P("expert", "dp", None)),
        check_vma=False,
    )
```

```python
import jax
import jax.numpy as jnp
from jax import lax
from jax.experimental import pallas as pl
from jax.experimental.pallas import tpu as pltpu
from jax.sharding import PartitionSpec as P

ROOT_TWO_PI = 0.7978845608028654
CUBIC = 0.044715
MESH = pl.DeviceIdType.MESH

SIDE = 8
PEERS = 64
RING = 8
TOK = 128
WIDTH = 2048
FF = 1024
CAP = 256
SLOTS = 6
FLAT = PEERS * SLOTS
SUB = 16
GROUP = 16
GROUPS = PEERS // GROUP
ROWS = GROUP * SLOTS
BLOCK = FF // (2 * RING)
HALF = BLOCK // 2

F32 = jnp.float32
BF16 = jnp.bfloat16
I32 = jnp.int32


def contract(left, right, left_dim, right_dim):
    return lax.dot_general(
        left, right, (((left_dim,), (right_dim,)), ((), ())), preferred_element_type=F32
    )


def gelu_pair(values):
    inner_arg = ROOT_TWO_PI * (values + CUBIC * values * values * values)
    tanh_part = jnp.tanh(inner_arg)
    hidden = 0.5 * values * (1.0 + tanh_part)
    slope_vals = 0.5 * (1.0 + tanh_part) + 0.5 * values * (
        1.0 - tanh_part * tanh_part
    ) * ROOT_TWO_PI * (1.0 + 3.0 * CUBIC * values * values)
    return hidden, slope_vals


def iota(shape, dim):
    return lax.broadcasted_iota(I32, shape, dim)


def kernel(
    choices_hbm, logits_hbm, rows_hbm, act_hbm, down_hbm, up_hbm,
    tok_out, logit_out, down_out,
    choices_ref, logits_ref, rows_ref, act_ref, w_down, w_up, tok_sum, stage, send_buf, recv_buf, back_buf, ret_buf,
    gate_send, gate_recv, grad_send, grad_recv,
    landing, tok_of_row, rows2d, scaled, hidden, slope, hidden_t, pre_grad,
    partial, pair_recv, pair_sum, ring_send, ring_recv,
    weight_sem,
    send_sem, recv_sem, gate_send_sem, gate_recv_sem,
    back_send_sem, back_recv_sem, grad_send_sem, grad_recv_sem,
    pair_send_sem, pair_recv_sem, ring_send_sem, ring_recv_sem,
):
    me = lax.axis_index("expert")
    data = lax.axis_index("dp")
    my_z, my_y = lax.div(me, SIDE), lax.rem(me, SIDE)
    my_x, core = lax.div(data, 2), lax.rem(data, 2)
    sign = 1 - 2 * core

    def partner(step, way):
        dz = lax.rem(3 * step, SIDE)
        dy = lax.rem(2 * step + lax.div(step, SIDE), SIDE)
        z = lax.rem(my_z + way * dz + SIDE, SIDE)
        y = lax.rem(my_y + way * dy + SIDE, SIDE)
        return z * SIDE + y

    def step_between(origin, target):
        dz = jnp.bitwise_and(sign * ((target >> 3) - (origin >> 3)), SIDE - 1)
        dy = jnp.bitwise_and(sign * ((target & 7) - (origin & 7)), SIDE - 1)
        low = jnp.bitwise_and(3 * dz, SIDE - 1)
        return jnp.bitwise_and(dy - 2 * low, SIDE - 1) * SIDE + low

    right = lax.rem(my_x + 1, RING) * 2 + core
    left = lax.rem(my_x + RING - 1, RING) * 2 + core
    sibling = my_x * 2 + 1 - core

    barrier = pltpu.get_barrier_semaphore()

    def greet(step, carry):
        pl.semaphore_signal(
            barrier, inc=1, device_id={"expert": lax.rem(me + step, PEERS)}, device_id_type=MESH
        )
        return carry

    lax.fori_loop(1, PEERS, greet, 0, unroll=9)
    for other in (left, right, sibling):
        pl.semaphore_signal(barrier, inc=1, device_id={"dp": other}, device_id_type=MESH)
    loads = [
        pltpu.make_async_copy(source, target, weight_sem.at[i])
        for i, (source, target) in enumerate(
            (
                (choices_hbm, choices_ref), (logits_hbm, logits_ref), (rows_hbm, rows_ref),
                (act_hbm, act_ref), (down_hbm, w_down), (up_hbm, w_up),
            )
        )
    ]
    for load in loads:
        load.start()
    loads[0].wait()

    chosen = choices_ref[...]
    mine = (chosen >> 7) == me
    token = jnp.where(mine, (chosen & (TOK - 1)) + 1, 0)
    lane = iota((PEERS, CAP), 1)
    before = jnp.where(mine, 1, 0)
    shift = 1
    while shift < CAP:
        before = before + jnp.where(lane >= shift, pltpu.roll(before, shift, 1), 0)
        shift *= 2
    column = iota((PEERS, GROUPS * 128), 1)
    within = column & 127
    step_in = (within * 43) >> 8
    slot_in = within - SLOTS * step_in
    at_step = step_between(me, iota((PEERS, GROUPS * 128), 0)) == (column >> 7) * GROUP + step_in
    at_step = at_step & (within < ROWS)
    spread = jnp.zeros((PEERS, GROUPS * 128), I32)
    for k in range(SLOTS):
        token_k = jnp.sum(jnp.where(before == k + 1, token, 0), axis=1, keepdims=True)
        spread = spread + jnp.where(at_step & (slot_in == k), token_k, 0)
    token_row = jnp.sum(spread, axis=0, keepdims=True) - 1
    landing_f = jnp.where(token_row == iota((TOK, GROUPS * 128), 0), 1.0, 0.0)
    landing[...] = landing_f.astype(BF16)

    expert_step = step_between(me, iota((PEERS, PEERS), 0)) == iota((PEERS, PEERS), 1)
    expert_to_step = jnp.where(expert_step, 1.0, 0.0).astype(BF16)
    loads[1].wait()
    gates = 1.0 / (1.0 + jnp.exp(-logits_ref[...]))
    gate_send[:, 0, :] = contract(expert_to_step, gates.astype(BF16), 0, 0)

    def tiles(row, count):
        return pl.ds(pl.multiple_of(row * SUB, SUB), count * SUB)

    def gather(g):
        pick = jnp.transpose(landing_f[:, g * 128:(g + 1) * 128]).astype(BF16)[0:ROWS]
        for n in range(WIDTH // 256):
            rows_n = jnp.dot(
                pick, rows_ref[:, n * 256:(n + 1) * 256], preferred_element_type=F32
            )
            for h in range(2):
                stage[pl.ds(g * ROWS * SUB + 2 * n + h, ROWS, stride=SUB), :] = rows_n[
                    :, h * 128:(h + 1) * 128
                ]

    def pack(row):
        return stage[tiles(row, SLOTS), :].astype(BF16).reshape(SLOTS, SUB, 128)

    def push(step, carry):
        block = pl.ds(step * SLOTS, SLOTS)
        send_buf[block] = pack(step * SLOTS)
        p = partner(step, sign)
        g = lax.div(step, GROUP)
        pltpu.make_async_remote_copy(
            src_ref=gate_send.at[pl.ds(step, 1)], dst_ref=gate_recv.at[pl.ds(step, 1)],
            send_sem=gate_send_sem, recv_sem=gate_recv_sem.at[g],
            device_id={"expert": p}, device_id_type=MESH,
        ).start()
        pltpu.make_async_remote_copy(
            src_ref=send_buf.at[block], dst_ref=recv_buf.at[block],
            send_sem=send_sem, recv_sem=recv_sem.at[g],
            device_id={"expert": p}, device_id_type=MESH,
        ).start()
        return carry

    loads[2].wait()
    gather(0)
    pl.semaphore_wait(barrier, PEERS + 2)
    lax.fori_loop(1, GROUP, push, 0)
    for g in range(1, GROUPS):
        gather(g)
        lax.fori_loop(g * GROUP, (g + 1) * GROUP, push, 0)
    recv_buf[0:SLOTS] = pack(0)
    gate_recv[0:1] = gate_send[0:1]

    own = iota((PEERS, CAP), 0) == me
    own_row = jnp.sum(jnp.where(own, chosen, 0), axis=0, keepdims=True)
    here, there = iota((CAP, CAP), 0), iota((CAP, CAP), 1)
    own_col = jnp.sum(jnp.where(here == there, own_row, 0), axis=1, keepdims=True)
    src_row, src_col = own_row >> 7, own_col >> 7
    loc_col = own_col & (TOK - 1)
    rank_col = jnp.sum(
        jnp.where((src_col == src_row) & (there < here), 1, 0), axis=1, keepdims=True
    )
    step_col = step_between(src_col, me)
    column_col = (step_col >> 4) * 128 + (step_col & (GROUP - 1)) * SLOTS + rank_col
    arrival = jnp.where(
        column_col == iota((CAP, GROUPS * 128), 1), 1.0, 0.0
    )
    onehot_loc = jnp.where(loc_col == iota((CAP, TOK), 1), 1.0, 0.0).astype(BF16)
    loads[3].wait()
    for g in range(GROUPS):
        block = slice(g * ROWS, (g + 1) * ROWS)
        place = jnp.transpose(arrival[:, g * 128:(g + 1) * 128]).astype(BF16)[0:ROWS]
        tok_of_row[block, :] = jnp.dot(place, onehot_loc, preferred_element_type=F32)
        for n in range(FF // 256):
            columns = slice(n * 256, (n + 1) * 256)
            act = jnp.dot(place, act_ref[:, columns], preferred_element_type=F32)
            hidden_n, slope_n = gelu_pair(act)
            hidden[block, columns] = hidden_n
            slope[block, columns] = slope_n
    for n in range(RING):
        turned = jnp.transpose(hidden[:, n * 128:(n + 1) * 128]).astype(BF16)
        hidden_t[pl.ds((1 - core) * (RING * BLOCK) + n * BLOCK, BLOCK), :] = turned[0:BLOCK]
        hidden_t[pl.ds(core * (RING * BLOCK) + n * BLOCK, BLOCK), :] = turned[BLOCK:]
    row_step = lax.div(iota((ROWS, GROUP), 0), SLOTS) == iota((ROWS, GROUP), 1)
    row_to_step = jnp.where(row_step, 1.0, 0.0).astype(BF16)

    def wait_bytes(source, target, sem, count):
        pltpu.make_async_copy(
            source.at[pl.ds(0, count)], target.at[pl.ds(0, count)], sem
        ).wait()

    def await_rows(g):
        steps = GROUP - 1 if g == 0 else GROUP
        wait_bytes(gate_send, gate_recv, gate_recv_sem.at[g], steps)
        wait_bytes(send_buf, recv_buf, recv_sem.at[g], steps * SLOTS)

    def unpack(source, g):
        for j in range(8):
            count = ROWS // 8
            stage[j * count * SUB:(j + 1) * count * SUB, :] = (
                source[g * ROWS + j * count:g * ROWS + (j + 1) * count]
                .astype(F32)
                .reshape(count * SUB, 128)
            )

    def arrive(g):
        block = slice(g * ROWS, (g + 1) * ROWS)
        unpack(recv_buf, g)
        gate_rows = jnp.dot(
            row_to_step,
            gate_recv[g * GROUP:(g + 1) * GROUP, 0, :].astype(BF16),
            preferred_element_type=F32,
        )
        gate_col = jnp.sum(gate_rows * tok_of_row[block, :], axis=1, keepdims=True)
        for c in range(SUB):
            columns = slice(c * 128, (c + 1) * 128)
            chunk = stage[pl.ds(c, ROWS, stride=SUB), :]
            rows2d[block, columns] = chunk.astype(BF16)
            scaled[block, columns] = (gate_col * chunk).astype(BF16)
        return gate_col

    def work(g, gate_col):
        block = slice(g * ROWS, (g + 1) * ROWS)
        gate_grad = jnp.zeros((ROWS, 1), F32)
        for n in range(FF // 256):
            columns = slice(n * 256, (n + 1) * 256)
            back = contract(rows2d[block, :], w_down[columns, :], 1, 1)
            gate_grad = gate_grad + jnp.sum(back * hidden[block, columns], axis=1, keepdims=True)
            pre_grad[:, columns] = (gate_col * back * slope[block, columns]).astype(BF16)
        marked = (gate_grad.astype(BF16).astype(F32) * tok_of_row[block, :]).astype(BF16)
        grad_send[g * GROUP:(g + 1) * GROUP, 0, :] = contract(row_to_step, marked, 0, 0)
        for n in range(WIDTH // 256):
            rows_n = contract(pre_grad[...], w_up[n * 256:(n + 1) * 256, :], 1, 1)
            for h in range(2):
                stage[pl.ds(2 * n + h, ROWS, stride=SUB), :] = rows_n[:, h * 128:(h + 1) * 128]
        for j in range(8):
            count = ROWS // 8
            back_buf[g * ROWS + j * count:g * ROWS + (j + 1) * count] = (
                stage[j * count * SUB:(j + 1) * count * SUB, :]
                .astype(BF16)
                .reshape(count, SUB, 128)
            )

    def push_back(step, carry):
        block = pl.ds(step * SLOTS, SLOTS)
        p = partner(step, -sign)
        g = lax.div(step, GROUP)
        pltpu.make_async_remote_copy(
            src_ref=grad_send.at[pl.ds(step, 1)], dst_ref=grad_recv.at[pl.ds(step, 1)],
            send_sem=grad_send_sem, recv_sem=grad_recv_sem.at[g],
            device_id={"expert": p}, device_id_type=MESH,
        ).start()
        pltpu.make_async_remote_copy(
            src_ref=back_buf.at[block], dst_ref=ret_buf.at[block],
            send_sem=back_send_sem, recv_sem=back_recv_sem.at[g],
            device_id={"expert": p}, device_id_type=MESH,
        ).start()
        return carry

    for g in range(GROUPS - 1):
        await_rows(g)
        gate_col = arrive(g)
        if g == 0:
            loads[4].wait()
            loads[5].wait()
        work(g, gate_col)
    lax.fori_loop(1, GROUP, push_back, 0)
    await_rows(GROUPS - 1)
    gate_col = arrive(GROUPS - 1)

    def multiply(half):
        rows = slice(half * RING * BLOCK, (half + 1) * RING * BLOCK)
        for n in range(WIDTH // 256):
            columns = slice(n * 256, (n + 1) * 256)
            partial[rows, columns] = jnp.dot(
                hidden_t[rows, :], scaled[:, columns], preferred_element_type=F32
            ).astype(BF16)

    away = (4, 3, -3, 2, -2, 1, -1, 0)

    def pair_copy(j):
        block = lax.rem(my_x + away[j] + RING, RING)
        return pltpu.make_async_remote_copy(
            src_ref=partial.at[pl.ds(block * BLOCK, BLOCK)],
            dst_ref=pair_recv.at[pl.ds(block * BLOCK, BLOCK)],
            send_sem=pair_send_sem, recv_sem=pair_recv_sem.at[j],
            device_id={"dp": sibling}, device_id_type=MESH,
        )

    def pair_add(j):
        pair_copy(j).wait_recv()
        block = lax.rem(my_x + away[j] + RING, RING)
        both = pair_recv[pl.ds(block * BLOCK, BLOCK), :].astype(F32) + partial[
            pl.ds((RING + block) * BLOCK, BLOCK), :
        ].astype(F32)
        pair_sum[pl.ds(block * BLOCK, BLOCK), :] = both.astype(BF16)

    multiply(0)
    for j in range(RING):
        pair_copy(j).start()
    multiply(1)
    lax.fori_loop(GROUP, (GROUPS - 1) * GROUP, push_back, 0)

    streams = ((0, 1, 4), (0, -1, 3), (1, 1, 3), (1, -1, 4))
    slot_of = {}
    for stream, (half, way, steps) in enumerate(streams):
        for s in range(1, steps + 1):
            slot_of[stream, s] = len(slot_of)

    def ring_copy(stream, s):
        half, way, steps = streams[stream]
        slot = slot_of[stream, s]
        block = lax.rem(my_x + way * (steps + 1 - s) + RING, RING)
        place = pl.ds(block * BLOCK + half * HALF, HALF)
        return place, slot, pltpu.make_async_remote_copy(
            src_ref=pair_sum.at[place] if s == 1 else ring_send.at[slot],
            dst_ref=ring_recv.at[slot],
            send_sem=ring_send_sem.at[slot], recv_sem=ring_recv_sem.at[slot],
            device_id={"dp": right if way == 1 else left}, device_id_type=MESH,
        )

    def ring_step(s):
        for stream, (half, way, steps) in enumerate(streams):
            if s > steps:
                continue
            place, slot, copy = ring_copy(stream, s)
            if s > 1:
                ring_copy(stream, s - 1)[2].wait_recv()
                total = ring_recv[slot_of[stream, s - 1]].astype(F32) + pair_sum[place, :].astype(F32)
                ring_send[slot] = total.astype(BF16)
            copy.start()

    def land(g):
        steps = GROUP - 1 if g == 0 else GROUP
        wait_bytes(grad_send, grad_recv, grad_recv_sem.at[g], steps)
        wait_bytes(back_buf, ret_buf, back_recv_sem.at[g], steps * SLOTS)
        unpack(ret_buf, g)
        for c in range(SUB):
            rows2d[g * ROWS:(g + 1) * ROWS, c * 128:(c + 1) * 128] = stage[
                pl.ds(c, ROWS, stride=SUB), :
            ].astype(BF16)

    for j in range(3):
        pair_add(j)
    ring_step(1)
    work(GROUPS - 1, gate_col)
    lax.fori_loop((GROUPS - 1) * GROUP, PEERS, push_back, 0)
    ret_buf[0:SLOTS] = back_buf[0:SLOTS]
    grad_recv[0:1] = grad_send[0:1]
    for j in range(3, RING):
        pair_add(j)
    ring_step(2)
    land(0)
    ring_step(3)
    land(1)
    ring_step(4)
    land(2)
    for half in range(2):
        place = pl.ds(my_x * BLOCK + half * HALF, HALF)
        total = pair_sum[place, :].astype(F32)
        for stream, (of_half, way, steps) in enumerate(streams):
            if of_half == half:
                ring_copy(stream, steps)[2].wait_recv()
                total = total + ring_recv[slot_of[stream, steps]].astype(F32)
        down_out[half * HALF:(half + 1) * HALF, :] = total.astype(BF16)
    def landed(g, columns):
        return jnp.dot(
            landing[:, g * 128:g * 128 + ROWS],
            rows2d[g * ROWS:(g + 1) * ROWS, columns],
            preferred_element_type=F32,
        )

    for n in range(WIDTH // 256):
        columns = slice(n * 256, (n + 1) * 256)
        tok_sum[:, columns] = landed(0, columns) + landed(1, columns) + landed(2, columns)
    land(3)
    for n in range(WIDTH // 256):
        columns = slice(n * 256, (n + 1) * 256)
        tok_out[:, columns] = (tok_sum[:, columns] + landed(3, columns)).astype(BF16)
    gates = 1.0 / (1.0 + jnp.exp(-logits_ref[...]))
    step_to_expert = jnp.where(
        step_between(me, iota((PEERS, PEERS), 1)) == iota((PEERS, PEERS), 0), 1.0, 0.0
    ).astype(BF16)
    picked_grad = contract(step_to_expert, grad_recv[:, 0, :].astype(BF16), 0, 0)
    logit_out[...] = picked_grad * gates * (1.0 - gates)

    others = FLAT - SLOTS
    wait_bytes(send_buf, recv_buf, send_sem, others)
    wait_bytes(gate_send, gate_recv, gate_send_sem, PEERS - 1)
    wait_bytes(back_buf, ret_buf, back_send_sem, others)
    wait_bytes(grad_send, grad_recv, grad_send_sem, PEERS - 1)
    wait_bytes(pair_sum, pair_recv, pair_send_sem, RING * BLOCK)
    for stream, s in slot_of:
        ring_copy(stream, s)[2].wait_send()


def hand_over(tokens, logits, down, tok_out, logit_out, down_out, sems):
    copies = [
        pltpu.make_async_copy(source, target, sems.at[i])
        for i, (source, target) in enumerate(
            ((tokens, tok_out), (logits, logit_out), (down, down_out))
        )
    ]
    for copy in copies:
        copy.start()
    for copy in copies:
        copy.wait()


def on_device(grad_out, router_logits, choices, pre_act, w_down, w_up):
    vmem = pl.BlockSpec(memory_space=pltpu.VMEM)
    anywhere = pl.BlockSpec(memory_space=pl.ANY)
    dma = pltpu.SemaphoreType.DMA
    tokens, logits, down = pl.pallas_call(
        kernel,
        out_shape=(
            pltpu.VMEM((TOK, WIDTH), BF16),
            pltpu.VMEM((PEERS, TOK), F32),
            pltpu.VMEM((BLOCK, WIDTH), BF16),
        ),
        in_specs=[anywhere] * 6,
        out_specs=(vmem, vmem, vmem),
        scratch_shapes=[
            pltpu.VMEM((PEERS, CAP), I32),
            pltpu.VMEM((PEERS, TOK), F32),
            pltpu.VMEM((TOK, WIDTH), BF16),
            pltpu.VMEM((CAP, FF), BF16),
            pltpu.VMEM((FF, WIDTH), BF16),
            pltpu.VMEM((WIDTH, FF), BF16),
            pltpu.VMEM((TOK, WIDTH), F32),
            pltpu.VMEM((FLAT * SUB, 128), F32),
            pltpu.VMEM((FLAT, SUB, 128), BF16),
            pltpu.VMEM((FLAT, SUB, 128), BF16),
            pltpu.VMEM((FLAT, SUB, 128), BF16),
            pltpu.VMEM((FLAT, SUB, 128), BF16),
            pltpu.VMEM((PEERS, 1, TOK), F32),
            pltpu.VMEM((PEERS, 1, TOK), F32),
            pltpu.VMEM((PEERS, 1, TOK), F32),
            pltpu.VMEM((PEERS, 1, TOK), F32),
            pltpu.VMEM((TOK, GROUPS * 128), BF16),
            pltpu.VMEM((FLAT, TOK), F32),
            pltpu.VMEM((FLAT, WIDTH), BF16),
            pltpu.VMEM((FLAT, WIDTH), BF16),
            pltpu.VMEM((FLAT, FF), F32),
            pltpu.VMEM((FLAT, FF), F32),
            pltpu.VMEM((FF, FLAT), BF16),
            pltpu.VMEM((ROWS, FF), BF16),
            pltpu.VMEM((FF, WIDTH), BF16),
            pltpu.VMEM((RING * BLOCK, WIDTH), BF16),
            pltpu.VMEM((RING * BLOCK, WIDTH), BF16),
            pltpu.VMEM((14, HALF, WIDTH), BF16),
            pltpu.VMEM((14, HALF, WIDTH), BF16),
            dma((6,)),
            dma, dma((GROUPS,)), dma, dma((GROUPS,)),
            dma, dma((GROUPS,)), dma, dma((GROUPS,)),
            dma, dma((RING,)), dma((14,)), dma((14,)),
        ],
        compiler_params=pltpu.CompilerParams(
            collective_id=0, has_side_effects=True, vmem_limit_bytes=54 << 20
        ),
        cost_estimate=pl.CostEstimate(
            flops=3 * 2 * CAP * FF * WIDTH, bytes_accessed=12 << 20, transcendentals=CAP * FF
        ),
        name="expert_backward",
    )(choices[0], router_logits[0].T, grad_out[0], pre_act[0, 0], w_down[0], w_up[0])
    tokens, logits, down = pl.pallas_call(
        hand_over,
        out_shape=[jax.ShapeDtypeStruct(x.shape, x.dtype) for x in (tokens, logits, down)],
        in_specs=[vmem] * 3,
        out_specs=[anywhere] * 3,
        scratch_shapes=[dma((3,))],
        name="hand_over",
    )(tokens, logits, down)
    return tokens[None], logits.T[None], down[None]


def solution(mesh):
    return jax.shard_map(
        on_device,
        mesh=mesh,
        in_specs=(
            P("dp", "expert", None),
            P("dp", "expert", None),
            P("dp", None, None),
            P("dp", "expert", None, None),
            P("expert", None, None),
            P("expert", None, None),
        ),
        out_specs=(P("dp", "expert", None), P("dp", "expert", None), P("expert", "dp", None)),
        check_vma=False,
    )
```
